256 devices in a mesh: grp: 4 (over z_hi, core), tile: 64 (over y, x, z_lo).
Axes of the slice: x: 4, y: 4, z: 8 (z_hi: 2, z_lo: 4; z = z_hi * 4 + z_lo), core: 2. Of those that a mesh axis runs over, the one named last changes fastest.
Arguments:
- fields: float32 [4, 4, 4096, 1024], P('grp', None, 'tile'), may hold values from -6 to 6
- face_aux: float32 [4, 2, 8, 4096], P('grp', None, None, 'tile'), may hold values from -6 to 6
- block_owner: int32 [4, 32768], P('grp', 'tile'), may hold values from -1 to 32767, as said below
Outputs:
- fields_out: float32 [4, 4, 4096, 1024], P('grp', None, 'tile')
- face_aux_out: float32 [4, 2, 8, 4096], P('grp', None, None, 'tile')
The draws below stay inside these ranges and needn't reach their ends.
Inputs may be any that keep to these rules, and one draw needn't show every extreme that they name: `block_owner`: the last group's entries are -1. Each LES device's blocks name at most 12 blocks of any one acoustic tile, and exactly 12 of one of them; several LES blocks may name the same acoustic block.
All inputs are finite; a program needn't handle non-finite values.
Results may differ from the reference program's by a relative error of at most 0.0008.
Values may be sent and summed in bfloat16 or wider, within the bound.
A program may use at most 64 MiB of HBM per device.

```python
import math
import jax
import jax.numpy as jnp
from jax import lax

CZ = 1024
BLK = 128
CAP = 12
AUX = 8
BLOCKS_DEV = 512
NX = 4096
N_GRP = 4
N_TILE = 64


def draw_block_owner(key, part):
    key = jax.random.fold_in(key, 7)
    keys = jax.random.split(key, 5)
    shape = (N_GRP, N_TILE, BLOCKS_DEV)
    weights = jax.random.randint(keys[0], (N_TILE,), 1, 5)
    bounds = jnp.cumsum(weights)
    pick = jax.random.randint(keys[1], shape, 0, bounds[-1])
    target = jnp.sum((pick[..., None] >= bounds).astype(jnp.int32), axis=-1)
    favoured = jax.random.randint(keys[2], (N_GRP, N_TILE, 1), 0, N_TILE)
    favoured = favoured.at[0, 0, 0].set(N_TILE - 1)
    leading = (jnp.arange(BLOCKS_DEV) < CAP)[None, None, :]
    target = jnp.where(leading, favoured, target)
    active = leading | (jax.random.randint(keys[3], shape, 0, 4) > 0)
    placed = jax.random.randint(keys[4], shape, 0, BLOCKS_DEV)
    placed = placed.at[0, 0, 0].set(BLOCKS_DEV - 1)
    hits = ((target[..., None] == jnp.arange(N_TILE)) & active[..., None]).astype(jnp.int32)
    before = jnp.cumsum(hits, axis=2) - hits
    rank = jnp.sum(before * hits, axis=-1)
    keep = active & (rank < CAP) & (jnp.arange(N_GRP)[:, None, None] < N_GRP - 1)
    owner = jnp.where(keep, target * BLOCKS_DEV + placed, -1)
    return owner.reshape(N_GRP, N_TILE * BLOCKS_DEV).astype(jnp.int32)


def shard_levels(own_key, shape, cuts, least, largest):
    def one(position, blocks):
        steps = jax.random.uniform(jax.random.fold_in(jax.random.fold_in(own_key, 6), position), (blocks,), jnp.float32, least / len(cuts), largest / len(cuts))
        return jnp.repeat(jnp.exp(steps), shape[position] // blocks).reshape((-1,) + (1,) * (len(shape) - position - 1))

    gain = one(*cuts[0])
    for cut in cuts[1:]:
        gain = gain * one(*cut)
    return gain


def centred(own_key, dims, scale, most, cuts=(), kind=jnp.bfloat16):
    level = shard_levels(own_key, dims, cuts, -0.22, 0.18) if cuts else 1.0
    entries = jax.random.normal(own_key, dims, jnp.float32) * scale * level
    return jnp.minimum(jnp.maximum(entries, -most), most).astype(kind)


def setup_inputs(seed: int = 0) -> dict:
    key_list = jax.random.split(jax.random.key(seed), 4)
    return {
        "fields": centred(key_list[0], (N_GRP, 4, NX, CZ), 1.0, 6.0, ((0, 4), (2, 64)), jnp.float32),
        "face_aux": centred(key_list[1], (N_GRP, 2, AUX, NX), 1.0, 6.0, ((0, 4), (3, 64)), jnp.float32),
        "block_owner": draw_block_owner(jax.random.fold_in(key_list[3], 71), 0),
    }


LES_DT = 0.1
VISCOSITY = 1.0
ACOUSTIC_DT = 0.2
MACH = 0.3
TANGENT = 1.0


def hw_tables(order):
    level = jnp.arange(order, dtype=jnp.float32)
    rates = 0.1 * (level + 1.0)
    coupling = jnp.cos(math.pi * (level + 0.5) / (2.0 * order)) ** 2
    return rates, coupling


def diff_rows(ext):
    return (ext[:, :-4] - 8.0 * ext[:, 1:-3] + 8.0 * ext[:, 3:-1] - ext[:, 4:]) / 12.0


def diff_depth(arr):
    padded = jnp.pad(arr, ((0, 0), (0, 0), (2, 2)))
    return (padded[:, :, :-4] - 8.0 * padded[:, :, 1:-3] + 8.0 * padded[:, :, 3:-1] - padded[:, :, 4:]) / 12.0


def les_substep(ext):
    core = ext[:, 2:-2]
    across = diff_rows(ext * ext[0:1])
    along = diff_depth(core * core[2:3])
    side = jnp.pad(core, ((0, 0), (0, 0), (1, 1)))
    lap = ext[:, 3:-1] + ext[:, 1:-3] + side[:, :, 2:] + side[:, :, :-2] - 4.0 * core
    return core - LES_DT * (across + along) + VISCOSITY * LES_DT * lap


def source_density(state):
    mix = state[0] * state[0] - state[2] * state[2] + state[1] * state[3]
    side = jnp.pad(mix, ((0, 0), (1, 1)))
    return 0.25 * side[:, :-2] + 0.5 * mix + 0.25 * side[:, 2:]


def ghost_diff(column, lower, upper):
    padded = jnp.concatenate([lower, lower, column, upper, upper], axis=1)
    return (padded[:, :-4] - 8.0 * padded[:, 1:-3] + 8.0 * padded[:, 3:-1] - padded[:, 4:]) / 12.0


def acoustic(ext, aux_ext, rates, coupling):
    core = ext[:, 2:-2]
    press, vel_x, vel_z, dens = core[0], core[1], core[2], core[3]
    out_low = 0.5 * (press[:, 0] - vel_z[:, 0])
    out_high = 0.5 * (press[:, -1] + vel_z[:, -1])
    outgoing = jnp.stack([out_low, out_high])
    aux = aux_ext[:, :, 1:-1]
    earlier = jnp.concatenate([outgoing[:, None], aux[:, :-1]], axis=1)
    second = aux_ext[:, :, 2:] + aux_ext[:, :, :-2] - 2.0 * aux
    aux_new = aux + ACOUSTIC_DT * (-rates[None, :, None] * aux + coupling[None, :, None] * (earlier - aux) + TANGENT * second)
    incoming = jnp.mean(aux_new, axis=1)
    p_low = (out_low + incoming[0])[:, None]
    p_high = (out_high + incoming[1])[:, None]
    w_low = (incoming[0] - out_low)[:, None]
    w_high = (out_high - incoming[1])[:, None]
    dz_press = ghost_diff(press, p_low, p_high)
    dz_vel = ghost_diff(vel_z, w_low, w_high)
    dx_all = diff_rows(ext)
    spread = dx_all[1] + dz_vel
    new_press = press + ACOUSTIC_DT * (-MACH * dx_all[0] - spread)
    new_vx = vel_x + ACOUSTIC_DT * (-MACH * dx_all[1] - dx_all[0])
    new_vz = vel_z + ACOUSTIC_DT * (-MACH * dx_all[2] - dz_press)
    new_dens = dens + ACOUSTIC_DT * (-MACH * dx_all[3] - spread)
    return jnp.stack([new_press, new_vx, new_vz, new_dens]), aux_new


def reference(fields, face_aux, block_owner):
    rates, coupling = hw_tables(AUX)
    dump = N_TILE * BLOCKS_DEV
    total = jnp.zeros((dump + 1, BLK), jnp.float32)
    les_states = []
    for group in range(N_GRP - 1):
        state = fields[group]
        for step in range(2):
            state = les_substep(jnp.pad(state, ((0, 0), (2, 2), (0, 0))))
        les_states.append(state)
        rounded = lax.optimization_barrier(source_density(state).reshape(-1, BLK).astype(jnp.bfloat16))
        owner = block_owner[group]
        target = jnp.where(owner < 0, dump, owner).astype(jnp.int32)
        total = total.at[target].add(rounded.astype(jnp.float32))
    source = total[:-1].reshape(NX, CZ)
    last = fields[N_GRP - 1]
    ext = jnp.pad(last, ((0, 0), (2, 2), (0, 0)))
    aux = face_aux[N_GRP - 1]
    aux_ext = jnp.concatenate([aux[:, :, -1:], aux, aux[:, :, :1]], axis=2)
    acoustic_state, aux_new = acoustic(ext, aux_ext, rates, coupling)
    acoustic_state = acoustic_state.at[0].add(ACOUSTIC_DT * source)
    fields_out = jnp.stack(les_states + [acoustic_state])
    face_aux_out = face_aux.at[N_GRP - 1].set(aux_new)
    return fields_out, face_aux_out
```

```python
import functools
import math

import jax
import jax.numpy as jnp
from jax import lax
from jax.experimental import pallas as pl
from jax.experimental.pallas import tpu as pltpu
from jax.sharding import PartitionSpec as P

MESH = pl.DeviceIdType.MESH
F32 = jnp.float32
BF16 = jnp.bfloat16

BLK = 128
SLOT = 16
HALO = 4

LES_DT = 0.1
VISCOSITY = 1.0
ACOUSTIC_DT = 0.2
MACH = 0.3
TANGENT = 1.0
NEAR = 8.0 * LES_DT / 12.0
FAR = LES_DT / 12.0
DIFF = VISCOSITY * LES_DT


def iota(shape, dim):
    return lax.broadcasted_iota(jnp.int32, shape, dim)


def exact_dot(a, b, dims):
    return lax.dot_general(
        a, b, (dims, ((), ())), precision=lax.Precision.HIGHEST, preferred_element_type=F32
    )


def roll(x, shift, axis):
    return pltpu.roll(x, shift % x.shape[axis], axis)


def ahead(one, two):
    lane, sub = iota((1, 8, BLK), 2), iota((1, 8, BLK), 1)
    one, two = roll(one, -1, 2), roll(two, -2, 2)
    own = jnp.where(lane < BLK - 1, one, 0.0) + jnp.where(lane < BLK - 2, two, 0.0)
    cross = jnp.where((lane == BLK - 1) & (sub > 0), one, 0.0) + jnp.where(
        (lane >= BLK - 2) & (sub > 0), two, 0.0
    )
    return own + roll(cross, -1, 1)


def behind(one, two):
    lane, sub = iota((1, 8, BLK), 2), iota((1, 8, BLK), 1)
    one, two = roll(one, 1, 2), roll(two, 2, 2)
    own = jnp.where(lane >= 1, one, 0.0) + jnp.where(lane >= 2, two, 0.0)
    cross = jnp.where((lane == 0) & (sub < 7), one, 0.0) + jnp.where(
        (lane < 2) & (sub < 7), two, 0.0
    )
    return own + roll(cross, 1, 1)


def rows_at(ref, part, row, count, span):
    start = pl.multiple_of((part * span + row) * 8, 8)
    return ref[pl.ds(start, count * 8), :].reshape(count, 8, BLK)


def put_rows(ref, part, row, value, span):
    start = pl.multiple_of((part * span + row) * 8, 8)
    ref[pl.ds(start, value.shape[0] * 8), :] = value.reshape(value.shape[0] * 8, BLK)


def les_rows(src, row, count, span):
    u = rows_at(src, 0, row - 2, count + 4, span)
    w = rows_at(src, 2, row, count, span)
    up, down, far = DIFF - NEAR * u[3:-1], DIFF + NEAR * u[1:-3], FAR * u
    right, left, side = DIFF - NEAR * w, DIFF + NEAR * w, FAR * w
    out = []
    for part in range(4):
        q = rows_at(src, part, row - 2, count + 4, span)
        core, bent = q[2:-2], far * q
        across = up * q[3:-1] + down * q[1:-3] + (bent[4:] - bent[:-4])
        edge = side * core
        along = ahead(right * core, edge) + behind(left * core, -edge)
        out.append((1.0 - 4.0 * DIFF) * core + across + along)
    return out


def source_rows(state):
    mix = state[0] * state[0] - state[2] * state[2] + state[1] * state[3]
    none = jnp.zeros_like(mix)
    quarter = 0.25 * mix
    return ahead(quarter, none) + behind(quarter, none) + 0.5 * mix


def slope_rows(q):
    return (q[:-4] - q[4:] + 8.0 * (q[3:-1] - q[1:-3])) * (1.0 / 12.0)


def slope_depth(q):
    near = (8.0 / 12.0) * q
    far = (1.0 / 12.0) * q
    return ahead(near, -far) + behind(-near, far)


def kernel(
    tiles, fields, face_aux, owner, out, aux_out,
    stage, state, middle, final, own, aux, aux_sides, halo_out, halo_in,
    pack, blocks, packed, ids, ids_in, ids_all, received, spread,
    load_sem, small_sem, halo_send, halo_recv, aux_send, aux_recv,
    id_send, id_recv, relay_send, relay_recv, relay_own, slot_send, slot_recv, ready,
):
    rows = stage.shape[1]
    span = rows + 2 * HALO
    group, tile = lax.axis_index("grp"), lax.axis_index("tile")
    last = lax.axis_size("grp") - 1
    after, before = lax.rem(tile + 1, tiles), lax.rem(tile + tiles - 1, tiles)
    is_les = group < last

    edges = (slice(0, 8), slice(rows - 8, rows), slice(8, rows - 8))
    loads = [
        pltpu.make_async_copy(fields.at[0, :, part], stage.at[:, part], load_sem.at[i])
        for i, part in enumerate(edges)
    ]
    own_load = pltpu.make_async_copy(owner, own, small_sem.at[0])
    aux_load = pltpu.make_async_copy(face_aux.at[0], aux, small_sem.at[1])

    barrier = pltpu.get_barrier_semaphore()
    for copy in loads:
        copy.start()
    aux_load.start()

    @pl.when(is_les)
    def _():
        own_load.start()
        for where in (before, after):
            pl.semaphore_signal(barrier, inc=1, device_id={"tile": where}, device_id_type=MESH)
        pl.semaphore_signal(barrier, inc=1, device_id={"grp": last}, device_id_type=MESH)

    @pl.when(group == last)
    def _():
        @pl.loop(1, tiles)
        def _(step):
            pl.semaphore_signal(
                barrier, inc=1, device_id={"tile": lax.rem(tile + step, tiles)}, device_id_type=MESH
            )

    def spread_rows(first, count):
        for part in range(4):
            for lane in range(8):
                start = (part * span + HALO + first) * 8 + lane
                state[pl.ds(start, count, stride=8), :] = stage[
                    part, first : first + count, lane * BLK : (lane + 1) * BLK
                ]

    loads[0].wait()
    loads[1].wait()
    spread_rows(0, 8)
    spread_rows(rows - 8, 8)
    for part in range(4):
        low = rows_at(state, part, HALO, HALO, span)
        high = rows_at(state, part, rows, HALO, span)
        halo_out[0, part * HALO * 8 : (part + 1) * HALO * 8] = low.reshape(-1, BLK).astype(BF16)
        halo_out[1, part * HALO * 8 : (part + 1) * HALO * 8] = high.reshape(-1, BLK).astype(BF16)

    @pl.when(is_les)
    def _():
        pl.semaphore_wait(barrier, 2)

    @pl.when(group == last)
    def _():
        pl.semaphore_wait(barrier, tiles - 1 + last)

    halos = [
        pltpu.make_async_remote_copy(
            halo_out.at[i], halo_in.at[i], halo_send.at[i], halo_recv.at[i],
            device_id={"tile": where}, device_id_type=MESH,
        )
        for i, where in ((0, before), (1, after))
    ]
    for copy in halos:
        copy.start()

    def take_halos():
        for copy in halos:
            copy.wait_recv()
        for part in range(4):
            piece = slice(part * HALO * 8, (part + 1) * HALO * 8)
            upper = jnp.where(tile == tiles - 1, 0.0, halo_in[0, piece].astype(F32))
            lower = jnp.where(tile == 0, 0.0, halo_in[1, piece].astype(F32))
            put_rows(state, part, 0, lower.reshape(HALO, 8, BLK), span)
            put_rows(state, part, rows + HALO, upper.reshape(HALO, 8, BLK), span)

    def send_halos():
        for copy in halos:
            copy.wait_send()

    def write_part(part):
        for lane in range(8):
            out[0, part, :, lane * BLK : (lane + 1) * BLK] = final[
                pl.ds(part * rows * 8 + lane, rows, stride=8), :
            ]

    @pl.when(is_les)
    def _():
        loads[2].wait()
        spread_rows(8, rows - 16)

        own_load.wait()
        count = own.shape[1]
        owned = own[...]
        live = owned >= 0
        target = lax.shift_right_logical(owned, int(math.log2(count)))
        place = jnp.bitwise_and(owned, count - 1)
        hit = (iota((tiles, count), 0) == target) & live
        hits = jnp.where(hit, 1.0, 0.0)
        earlier = jnp.where(iota((count, count), 0) < iota((count, count), 1), 1.0, 0.0)
        ranks = jnp.dot(hits.astype(BF16), earlier.astype(BF16), preferred_element_type=F32)
        rank = jnp.sum(hits * ranks, axis=0, keepdims=True).astype(jnp.int32)
        slot = jnp.where(live, target * SLOT + rank, -1)
        pack[...] = jnp.where(iota((tiles * SLOT, count), 0) == slot, 1.0, 0.0).astype(BF16)
        high = jnp.where(hit, lax.shift_right_logical(place, 4).astype(F32), 0.0)
        low = jnp.where(hit, (jnp.bitwise_and(place, 15) + 1).astype(F32), 0.0)
        column = rank + lax.rem(tile, 8) * SLOT
        chosen = jnp.where(iota((BLK, count), 0) == column, 1.0, 0.0).astype(BF16)
        digits = lax.dot_general(
            jnp.concatenate([high, low], axis=0).astype(BF16), chosen,
            (((1,), (1,)), ((), ())), preferred_element_type=F32,
        )
        ids[...] = (16.0 * digits[:tiles] + digits[tiles:]).reshape(tiles, 1, BLK)

        def first_step(row, size):
            for part, value in enumerate(les_rows(state, row, size, span)):
                put_rows(middle, part, row, value, span)

        def second_step(row, size):
            values = les_rows(middle, row, size, span)
            for part, value in enumerate(values):
                put_rows(final, part, row - HALO, value, rows)
            start = pl.multiple_of((row - HALO) * 8, 32)
            blocks[pl.ds(start, size * 8), :] = source_rows(values).reshape(-1, BLK).astype(BF16)

        @pl.loop(0, (rows - 4) // 4)
        def _(step):
            first_step(6 + step * 4, 4)

        @pl.loop(0, (rows - 8) // 4)
        def _(step):
            second_step(8 + step * 4, 4)

        pl.semaphore_wait(ready, 1)
        id_copy = pltpu.make_async_remote_copy(
            ids, ids_in.at[group], id_send, id_recv.at[group],
            device_id={"grp": last}, device_id_type=MESH,
        )
        id_copy.start()

        take_halos()
        first_step(2, 4)
        first_step(rows + 2, 4)
        for part in range(4):
            low_rows = rows_at(middle, part, 2, 2, span)
            put_rows(middle, part, 2, jnp.where(tile == 0, 0.0, low_rows), span)
            high_rows = rows_at(middle, part, rows + 4, 2, span)
            put_rows(middle, part, rows + 4, jnp.where(tile == tiles - 1, 0.0, high_rows), span)
        second_step(4, 4)
        second_step(rows, 4)

        chosen_blocks = jnp.dot(pack[...], blocks[...], preferred_element_type=F32)
        packed[...] = chosen_blocks.astype(BF16).reshape(tiles, SLOT, BLK)

        @pl.loop(0, tiles)
        def _(step):
            where = lax.rem(tile + step, tiles)
            pltpu.make_async_remote_copy(
                packed.at[where], received.at[group, tile], slot_send, slot_recv.at[group],
                device_id={"grp": last, "tile": where}, device_id_type=MESH,
            ).start()

        for part in range(4):
            write_part(part)
        aux_load.wait()
        aux_out[0] = aux[...]
        send_halos()
        id_copy.wait_send()
        pltpu.make_async_copy(packed, packed, slot_send).wait()

    @pl.when(group == last)
    def _():
        for part in range(3):
            pl.semaphore_signal(ready, inc=1, device_id={"grp": part}, device_id_type=MESH)
        aux_load.wait()
        turns = [
            pltpu.make_async_remote_copy(
                aux, aux_sides.at[i], aux_send.at[i], aux_recv.at[i],
                device_id={"tile": where}, device_id_type=MESH,
            )
            for i, where in ((0, before), (1, after))
        ]
        for copy in turns:
            copy.start()
        loads[2].wait()
        spread_rows(8, rows - 16)
        take_halos()

        dt = ACOUSTIC_DT

        @pl.loop(0, rows // 4)
        def _(step):
            row = HALO + step * 4
            p, u, w, r = (rows_at(state, part, row - 2, 8, span) for part in range(4))
            dp, du, dw, dr = (slope_rows(q) for q in (p, u, w, r))
            p, u, w, r = (q[2:-2] for q in (p, u, w, r))
            div = du + slope_depth(w)
            news = (
                p + dt * (-MACH * dp - div),
                u + dt * (-MACH * du - dp),
                w + dt * (-MACH * dw - slope_depth(p)),
                r + dt * (-MACH * dr - div),
            )
            for part, value in enumerate(news):
                put_rows(final, part, step * 4, value, rows)

        for copy in turns:
            copy.wait_recv()
        order = aux.shape[1]
        level = iota((order, 1), 0).astype(F32)
        rates = 0.1 * (level + 1.0)
        coupling = 0.5 + 0.5 * jnp.cos(math.pi * (level + 0.5) / order)
        here, there = iota((rows, rows), 0), iota((rows, rows), 1)
        bend = jnp.where(here == there, -2.0, 0.0) + jnp.where(
            (here == there + 1) | (here == there - 1), 1.0, 0.0
        )
        from_after = jnp.where((here == 0) & (there == rows - 1), 1.0, 0.0)
        from_before = jnp.where((here == rows - 1) & (there == 0), 1.0, 0.0)
        lane = iota((8, BLK), 1)
        kind = iota((8, BLK), 0)
        fixes = []
        for face in range(2):
            column = slice(0, BLK) if face == 0 else slice(7 * BLK, 8 * BLK)
            press, vel = stage[0, :, column], stage[2, :, column]
            mixed = 0.5 * (press - vel) if face == 0 else 0.5 * (press + vel)
            pick = jnp.where(lane == (0 if face == 0 else BLK - 1), 1.0, 0.0)
            outgoing = exact_dot(pick, mixed, ((1,), (1,)))[0:1]
            old = aux[face]
            second = (
                exact_dot(old, bend, ((1,), (0,)))
                + exact_dot(aux_sides[0, face], from_after, ((1,), (0,)))
                + exact_dot(aux_sides[1, face], from_before, ((1,), (0,)))
            )
            prior = jnp.concatenate([outgoing, old[:-1]], axis=0)
            new = old + dt * (-rates * old + coupling * (prior - old) + TANGENT * second)
            aux_out[0, face] = new
            incoming = jnp.sum(new, axis=0, keepdims=True) * (1.0 / order)
            ghost_p = outgoing + incoming
            ghost_w = incoming - outgoing if face == 0 else outgoing - incoming
            if face == 0:
                shape = jnp.where(lane == 0, -7.0 / 12.0, 0.0) + jnp.where(lane == 1, 1.0 / 12.0, 0.0)
            else:
                shape = jnp.where(lane == BLK - 1, 7.0 / 12.0, 0.0) + jnp.where(
                    lane == BLK - 2, -1.0 / 12.0, 0.0
                )
            shape = jnp.where(kind == 0, -dt * shape, 0.0)
            wide = [jnp.broadcast_to(g, (8, rows)) for g in (ghost_p, ghost_w)]
            fixes.append([exact_dot(g, shape, ((0,), (0,))) for g in wide])

        def fix(part, which):
            for face, column in ((0, slice(0, BLK)), (1, slice(7 * BLK, 8 * BLK))):
                out[0, part, :, column] = out[0, part, :, column] + fixes[face][which]

        for part in range(1, 4):
            write_part(part)
        fix(2, 0)
        fix(3, 1)

        for part in range(3):
            pltpu.make_async_copy(ids_in.at[part], ids_in.at[part], id_recv.at[part]).wait()
        mine = pltpu.make_async_copy(ids_in.at[:, tile], ids_all.at[:, tile], relay_own)
        mine.start()

        @pl.loop(1, tiles)
        def _(step):
            where = lax.rem(tile + step, tiles)
            pltpu.make_async_remote_copy(
                ids_in.at[:, where], ids_all.at[:, tile], relay_send, relay_recv,
                device_id={"tile": where}, device_id_type=MESH,
            ).start()

        mine.wait()
        others = ids_all.at[:, pl.ds(0, tiles - 1)]
        pltpu.make_async_copy(others, others, relay_recv).wait()
        count = spread.shape[0]
        for part in range(3):
            names = ids_all[part].reshape(tiles // 8, 8, BLK)
            names = jnp.sum(names, axis=1).astype(jnp.int32) - 1
            for piece in range(tiles // 8):
                start = (part * (tiles // 8) + piece) * BLK
                match = iota((count, BLK), 0) == names[piece : piece + 1]
                spread[:, start : start + BLK] = jnp.where(match, 1.0, 0.0).astype(BF16)
        pltpu.make_async_copy(others, others, relay_send).wait()
        for copy in turns:
            copy.wait_send()
        send_halos()

        total = jnp.zeros((count, BLK), F32)
        for part in range(3):
            got = received.at[part]
            pltpu.make_async_copy(got, got, slot_recv.at[part]).wait()
            width = tiles * SLOT
            total += jnp.dot(
                spread[:, part * width : (part + 1) * width],
                received[part].reshape(width, BLK), preferred_element_type=F32,
            )
        final[0:count, :] = final[0:count, :] + dt * total
        write_part(0)
        fix(0, 1)


def shards(tiles, fields, face_aux, block_owner):
    _, parts, rows, depth = fields.shape
    order = face_aux.shape[2]
    count = rows * depth // BLK
    span = rows + 2 * HALO
    vmem = pl.BlockSpec(memory_space=pltpu.VMEM)
    anywhere = pl.BlockSpec(memory_space=pl.ANY)
    dma = pltpu.SemaphoreType.DMA
    return pl.pallas_call(
        functools.partial(kernel, tiles),
        out_shape=(
            jax.ShapeDtypeStruct(fields.shape, F32),
            jax.ShapeDtypeStruct(face_aux.shape, F32),
        ),
        in_specs=[anywhere] * 3,
        out_specs=(vmem, vmem),
        scratch_shapes=[
            pltpu.VMEM((parts, rows, depth), F32),
            pltpu.VMEM((parts * span * 8, BLK), F32),
            pltpu.VMEM((parts * span * 8, BLK), F32),
            pltpu.VMEM((parts * rows * 8, BLK), F32),
            pltpu.VMEM((1, count), jnp.int32),
            pltpu.VMEM((2, order, rows), F32),
            pltpu.VMEM((2, 2, order, rows), F32),
            pltpu.VMEM((2, parts * HALO * 8, BLK), BF16),
            pltpu.VMEM((2, parts * HALO * 8, BLK), BF16),
            pltpu.VMEM((tiles * SLOT, count), BF16),
            pltpu.VMEM((count, BLK), BF16),
            pltpu.VMEM((tiles, SLOT, BLK), BF16),
            pltpu.VMEM((tiles, 1, BLK), F32),
            pltpu.VMEM((3, tiles, 1, BLK), F32),
            pltpu.VMEM((3, tiles, 1, BLK), F32),
            pltpu.VMEM((3, tiles, SLOT, BLK), BF16),
            pltpu.VMEM((count, 3 * tiles * SLOT), BF16),
            dma((3,)), dma((2,)), dma((2,)), dma((2,)), dma((2,)), dma((2,)),
            dma, dma((3,)), dma, dma, dma, dma, dma((3,)),
            pltpu.SemaphoreType.REGULAR,
        ],
        compiler_params=pltpu.CompilerParams(
            collective_id=0, has_side_effects=True, vmem_limit_bytes=40 << 20
        ),
    )(fields, face_aux, block_owner)


def solution(mesh):
    return jax.shard_map(
        functools.partial(shards, mesh.shape["tile"]),
        mesh=mesh,
        in_specs=(P("grp", None, "tile", None), P("grp", None, None, "tile"), P("grp", "tile")),
        out_specs=(P("grp", None, "tile", None), P("grp", None, None, "tile")),
        check_vma=False,
    )
```

```python
import functools
import math

import jax
import jax.numpy as jnp
from jax import lax
from jax.experimental import pallas as pl
from jax.experimental.pallas import tpu as pltpu
from jax.sharding import PartitionSpec as P

MESH = pl.DeviceIdType.MESH
F32 = jnp.float32
BF16 = jnp.bfloat16

BLK = 128
SLOT = 12
LANES = 16
CHUNKS = 4
WAVES = 2
HALO = 4

LES_DT = 0.1
VISCOSITY = 1.0
ACOUSTIC_DT = 0.2
MACH = 0.3
TANGENT = 1.0
NEAR = 8.0 * LES_DT / 12.0
FAR = LES_DT / 12.0
DIFF = VISCOSITY * LES_DT


def iota(shape, dim):
    return lax.broadcasted_iota(jnp.int32, shape, dim)


def exact_dot(a, b, dims):
    return lax.dot_general(
        a, b, (dims, ((), ())), precision=lax.Precision.HIGHEST, preferred_element_type=F32
    )


def roll(x, shift, axis):
    return pltpu.roll(x, shift % x.shape[axis], axis)


def ahead(one, two):
    lane, sub = iota((1, 8, BLK), 2), iota((1, 8, BLK), 1)
    one, two = roll(one, -1, 2), roll(two, -2, 2)
    own = jnp.where(lane < BLK - 1, one, 0.0) + jnp.where(lane < BLK - 2, two, 0.0)
    cross = jnp.where((lane == BLK - 1) & (sub > 0), one, 0.0) + jnp.where(
        (lane >= BLK - 2) & (sub > 0), two, 0.0
    )
    return own + roll(cross, -1, 1)


def behind(one, two):
    lane, sub = iota((1, 8, BLK), 2), iota((1, 8, BLK), 1)
    one, two = roll(one, 1, 2), roll(two, 2, 2)
    own = jnp.where(lane >= 1, one, 0.0) + jnp.where(lane >= 2, two, 0.0)
    cross = jnp.where((lane == 0) & (sub < 7), one, 0.0) + jnp.where(
        (lane < 2) & (sub < 7), two, 0.0
    )
    return own + roll(cross, 1, 1)


def rows_at(ref, part, row, count, span):
    start = pl.multiple_of((part * span + row) * 8, 8)
    return ref[pl.ds(start, count * 8), :].reshape(count, 8, BLK)


def put_rows(ref, part, row, value, span):
    start = pl.multiple_of((part * span + row) * 8, 8)
    ref[pl.ds(start, value.shape[0] * 8), :] = value.reshape(value.shape[0] * 8, BLK)


def les_rows(src, row, count, span):
    u = rows_at(src, 0, row - 2, count + 4, span)
    w = rows_at(src, 2, row, count, span)
    up, down, far = DIFF - NEAR * u[3:-1], DIFF + NEAR * u[1:-3], FAR * u
    right, left, side = DIFF - NEAR * w, DIFF + NEAR * w, FAR * w
    out = []
    for part in range(4):
        q = rows_at(src, part, row - 2, count + 4, span)
        core, bent = q[2:-2], far * q
        across = up * q[3:-1] + down * q[1:-3] + (bent[4:] - bent[:-4])
        edge = side * core
        along = ahead(right * core, edge) + behind(left * core, -edge)
        out.append((1.0 - 4.0 * DIFF) * core + across + along)
    return out


def source_rows(state):
    mix = state[0] * state[0] - state[2] * state[2] + state[1] * state[3]
    none = jnp.zeros_like(mix)
    quarter = 0.25 * mix
    return ahead(quarter, none) + behind(quarter, none) + 0.5 * mix


def slope_rows(q):
    return (q[:-4] - q[4:] + 8.0 * (q[3:-1] - q[1:-3])) * (1.0 / 12.0)


def slope_depth(q):
    near = (8.0 / 12.0) * q
    far = (1.0 / 12.0) * q
    return ahead(near, -far) + behind(-near, far)


def kernel(
    tiles, fields, face_aux, owner, out, aux_out,
    stage, state, middle, final, own, aux, aux_sides, halo_out, halo_in,
    pack, blocks, packed, ids, ids_in, ids_all, received, spread,
    load_sem, small_sem, halo_send, halo_recv, aux_send, aux_recv,
    id_send, id_recv, relay_send, relay_recv, relay_own, slot_send, slot_recv, ready,
):
    rows = stage.shape[1]
    span = rows + 2 * HALO
    group, tile = lax.axis_index("grp"), lax.axis_index("tile")
    last = lax.axis_size("grp") - 1
    after, before = lax.rem(tile + 1, tiles), lax.rem(tile + tiles - 1, tiles)
    is_les = group < last

    edges = (slice(0, 8), slice(rows - 8, rows), slice(8, rows - 8))
    loads = [
        pltpu.make_async_copy(fields.at[0, :, part], stage.at[:, part], load_sem.at[i])
        for i, part in enumerate(edges)
    ]
    own_load = pltpu.make_async_copy(owner, own, small_sem.at[0])
    aux_load = pltpu.make_async_copy(face_aux.at[0], aux, small_sem.at[1])

    barrier = pltpu.get_barrier_semaphore()
    for copy in loads:
        copy.start()
    aux_load.start()

    @pl.when(is_les)
    def _():
        own_load.start()
        for where in (before, after):
            pl.semaphore_signal(barrier, inc=1, device_id={"tile": where}, device_id_type=MESH)
        pl.semaphore_signal(barrier, inc=1, device_id={"grp": last}, device_id_type=MESH)

    @pl.when(group == last)
    def _():
        @pl.loop(1, tiles)
        def _(step):
            pl.semaphore_signal(
                barrier, inc=1, device_id={"tile": lax.rem(tile + step, tiles)}, device_id_type=MESH
            )

    def spread_rows(first, count):
        for part in range(4):
            for lane in range(8):
                start = (part * span + HALO + first) * 8 + lane
                state[pl.ds(start, count, stride=8), :] = stage[
                    part, first : first + count, lane * BLK : (lane + 1) * BLK
                ]

    loads[0].wait()
    loads[1].wait()
    spread_rows(0, 8)
    spread_rows(rows - 8, 8)
    for part in range(4):
        low = rows_at(state, part, HALO, HALO, span)
        high = rows_at(state, part, rows, HALO, span)
        halo_out[0, part * HALO * 8 : (part + 1) * HALO * 8] = low.reshape(-1, BLK).astype(BF16)
        halo_out[1, part * HALO * 8 : (part + 1) * HALO * 8] = high.reshape(-1, BLK).astype(BF16)

    @pl.when(is_les)
    def _():
        pl.semaphore_wait(barrier, 2)

    @pl.when(group == last)
    def _():
        pl.semaphore_wait(barrier, tiles - 1 + last)

    halos = [
        pltpu.make_async_remote_copy(
            halo_out.at[i], halo_in.at[i], halo_send.at[i], halo_recv.at[i],
            device_id={"tile": where}, device_id_type=MESH,
        )
        for i, where in ((0, before), (1, after))
    ]
    for copy in halos:
        copy.start()

    def take_halos():
        for copy in halos:
            copy.wait_recv()
        for part in range(4):
            piece = slice(part * HALO * 8, (part + 1) * HALO * 8)
            upper = jnp.where(tile == tiles - 1, 0.0, halo_in[0, piece].astype(F32))
            lower = jnp.where(tile == 0, 0.0, halo_in[1, piece].astype(F32))
            put_rows(state, part, 0, lower.reshape(HALO, 8, BLK), span)
            put_rows(state, part, rows + HALO, upper.reshape(HALO, 8, BLK), span)

    def send_halos():
        for copy in halos:
            copy.wait_send()

    def write_part(part):
        for lane in range(8):
            out[0, part, :, lane * BLK : (lane + 1) * BLK] = final[
                pl.ds(part * rows * 8 + lane, rows, stride=8), :
            ]

    @pl.when(is_les)
    def _():
        loads[2].wait()
        spread_rows(8, rows - 16)

        own_load.wait()
        count = own.shape[1]
        owned = own[...]
        live = owned >= 0
        target = lax.shift_right_logical(owned, int(math.log2(count)))
        place = jnp.bitwise_and(owned, count - 1)
        hit = (iota((tiles, count), 0) == target) & live
        hits = jnp.where(hit, 1.0, 0.0)
        earlier = jnp.where(iota((count, count), 0) < iota((count, count), 1), 1.0, 0.0)
        ranks = jnp.dot(hits.astype(BF16), earlier.astype(BF16), preferred_element_type=F32)
        rank = jnp.sum(hits * ranks, axis=0, keepdims=True).astype(jnp.int32)
        turn = jnp.bitwise_and(target - tile, tiles - 1)
        slot = jnp.where(live, turn * SLOT + rank, -1)
        pack[...] = jnp.where(iota((tiles * SLOT, count), 0) == slot, 1.0, 0.0).astype(BF16)
        high = jnp.where(hit, lax.shift_right_logical(place, 4).astype(F32), 0.0)
        low = jnp.where(hit, (jnp.bitwise_and(place, 15) + 1).astype(F32), 0.0)
        column = rank + group * LANES
        chosen = jnp.where(iota((BLK, count), 0) == column, 1.0, 0.0).astype(BF16)
        digits = lax.dot_general(
            jnp.concatenate([high, low], axis=0).astype(BF16), chosen,
            (((1,), (1,)), ((), ())), preferred_element_type=F32,
        )
        ids[...] = (16.0 * digits[:tiles] + digits[tiles:]).reshape(tiles, 1, BLK)

        def first_step(row, size):
            for part, value in enumerate(les_rows(state, row, size, span)):
                put_rows(middle, part, row, value, span)

        def second_step(row, size):
            values = les_rows(middle, row, size, span)
            for part, value in enumerate(values):
                put_rows(final, part, row - HALO, value, rows)
            start = pl.multiple_of((row - HALO) * 8, 32)
            blocks[pl.ds(start, size * 8), :] = source_rows(values).reshape(-1, BLK).astype(BF16)

        @pl.loop(0, (rows - 4) // 4)
        def _(step):
            first_step(6 + step * 4, 4)

        @pl.loop(0, (rows - 8) // 4)
        def _(step):
            second_step(8 + step * 4, 4)

        pl.semaphore_wait(ready, 1)
        id_copy = pltpu.make_async_remote_copy(
            ids, ids_in.at[group], id_send, id_recv.at[group],
            device_id={"grp": last}, device_id_type=MESH,
        )
        id_copy.start()

        take_halos()
        first_step(2, 4)
        first_step(rows + 2, 4)
        for part in range(4):
            low_rows = rows_at(middle, part, 2, 2, span)
            put_rows(middle, part, 2, jnp.where(tile == 0, 0.0, low_rows), span)
            high_rows = rows_at(middle, part, rows + 4, 2, span)
            put_rows(middle, part, rows + 4, jnp.where(tile == tiles - 1, 0.0, high_rows), span)
        second_step(4, 4)
        second_step(rows, 4)

        turns = tiles // CHUNKS
        for chunk in range(CHUNKS):
            first = chunk * turns
            chosen_blocks = jnp.dot(
                pack[first * SLOT : (first + turns) * SLOT], blocks[...], preferred_element_type=F32
            )
            packed[first : first + turns] = chosen_blocks.astype(BF16).reshape(
                turns, SLOT // 2, 2, BLK
            )
            wave = first * WAVES // tiles

            @pl.loop(first, first + turns)
            def _(step):
                pltpu.make_async_remote_copy(
                    packed.at[step], received.at[group, step], slot_send,
                    slot_recv.at[group, wave],
                    device_id={"grp": last, "tile": lax.rem(tile + step, tiles)},
                    device_id_type=MESH,
                ).start()

        for part in range(4):
            write_part(part)
        aux_load.wait()
        aux_out[0] = aux[...]
        send_halos()
        id_copy.wait_send()
        pltpu.make_async_copy(packed, packed, slot_send).wait()

    @pl.when(group == last)
    def _():
        for part in range(3):
            pl.semaphore_signal(ready, inc=1, device_id={"grp": part}, device_id_type=MESH)
        aux_load.wait()
        turns = [
            pltpu.make_async_remote_copy(
                aux, aux_sides.at[i], aux_send.at[i], aux_recv.at[i],
                device_id={"tile": where}, device_id_type=MESH,
            )
            for i, where in ((0, before), (1, after))
        ]
        for copy in turns:
            copy.start()
        loads[2].wait()
        spread_rows(8, rows - 16)
        take_halos()

        dt = ACOUSTIC_DT

        @pl.loop(0, rows // 4)
        def _(step):
            row = HALO + step * 4
            p, u, w, r = (rows_at(state, part, row - 2, 8, span) for part in range(4))
            dp, du, dw, dr = (slope_rows(q) for q in (p, u, w, r))
            p, u, w, r = (q[2:-2] for q in (p, u, w, r))
            div = du + slope_depth(w)
            news = (
                p + dt * (-MACH * dp - div),
                u + dt * (-MACH * du - dp),
                w + dt * (-MACH * dw - slope_depth(p)),
                r + dt * (-MACH * dr - div),
            )
            for part, value in enumerate(news):
                put_rows(final, part, step * 4, value, rows)

        for copy in turns:
            copy.wait_recv()
        order = aux.shape[1]
        level = iota((order, 1), 0).astype(F32)
        rates = 0.1 * (level + 1.0)
        coupling = 0.5 + 0.5 * jnp.cos(math.pi * (level + 0.5) / order)
        here, there = iota((rows, rows), 0), iota((rows, rows), 1)
        bend = jnp.where(here == there, -2.0, 0.0) + jnp.where(
            (here == there + 1) | (here == there - 1), 1.0, 0.0
        )
        from_after = jnp.where((here == 0) & (there == rows - 1), 1.0, 0.0)
        from_before = jnp.where((here == rows - 1) & (there == 0), 1.0, 0.0)
        lane = iota((8, BLK), 1)
        kind = iota((8, BLK), 0)
        fixes = []
        for face in range(2):
            column = slice(0, BLK) if face == 0 else slice(7 * BLK, 8 * BLK)
            press, vel = stage[0, :, column], stage[2, :, column]
            mixed = 0.5 * (press - vel) if face == 0 else 0.5 * (press + vel)
            pick = jnp.where(lane == (0 if face == 0 else BLK - 1), 1.0, 0.0)
            outgoing = exact_dot(pick, mixed, ((1,), (1,)))[0:1]
            old = aux[face]
            second = (
                exact_dot(old, bend, ((1,), (0,)))
                + exact_dot(aux_sides[0, face], from_after, ((1,), (0,)))
                + exact_dot(aux_sides[1, face], from_before, ((1,), (0,)))
            )
            prior = jnp.concatenate([outgoing, old[:-1]], axis=0)
            new = old + dt * (-rates * old + coupling * (prior - old) + TANGENT * second)
            aux_out[0, face] = new
            incoming = jnp.sum(new, axis=0, keepdims=True) * (1.0 / order)
            ghost_p = outgoing + incoming
            ghost_w = incoming - outgoing if face == 0 else outgoing - incoming
            if face == 0:
                shape = jnp.where(lane == 0, -7.0 / 12.0, 0.0) + jnp.where(lane == 1, 1.0 / 12.0, 0.0)
            else:
                shape = jnp.where(lane == BLK - 1, 7.0 / 12.0, 0.0) + jnp.where(
                    lane == BLK - 2, -1.0 / 12.0, 0.0
                )
            shape = jnp.where(kind == 0, -dt * shape, 0.0)
            wide = [jnp.broadcast_to(g, (8, rows)) for g in (ghost_p, ghost_w)]
            fixes.append([exact_dot(g, shape, ((0,), (0,))) for g in wide])

        def fix(part, which):
            for face, column in ((0, slice(0, BLK)), (1, slice(7 * BLK, 8 * BLK))):
                out[0, part, :, column] = out[0, part, :, column] + fixes[face][which]

        for part in range(1, 4):
            write_part(part)
        fix(2, 0)
        fix(3, 1)

        for part in range(3):
            pltpu.make_async_copy(ids_in.at[part], ids_in.at[part], id_recv.at[part]).wait()
        ids[...] = ids_in[0] + ids_in[1] + ids_in[2]
        mine = pltpu.make_async_copy(ids.at[tile], ids_all.at[0], relay_own)
        mine.start()

        @pl.loop(1, tiles)
        def _(step):
            where = lax.rem(tile + step, tiles)
            pltpu.make_async_remote_copy(
                ids.at[where], ids_all.at[step], relay_send, relay_recv,
                device_id={"tile": where}, device_id_type=MESH,
            ).start()

        mine.wait()
        others = ids_all.at[pl.ds(1, tiles - 1)]
        pltpu.make_async_copy(others, others, relay_recv).wait()
        count, width = spread.shape[1:]
        listed = ids_all[...].reshape(tiles, BLK)
        item = iota((1, tiles * SLOT), 1)
        turn = lax.shift_right_logical(item * 43691, 19)
        rank = item - turn * SLOT
        for part in range(3):
            column = jnp.where(iota((BLK, tiles * SLOT), 0) == rank + part * LANES, 1.0, 0.0)
            names = exact_dot(listed, column, ((1,), (0,)))
            names = jnp.where(iota((tiles, tiles * SLOT), 0) == turn, names, 0.0)
            names = jnp.sum(names, axis=0, keepdims=True).astype(jnp.int32) - 1
            for piece in range(tiles * SLOT // BLK):
                lanes = slice(piece * BLK, (piece + 1) * BLK)
                match = iota((count, BLK), 0) == names[:, lanes]
                spread[part, :, lanes] = jnp.where(match, 1.0, 0.0).astype(BF16)
        pltpu.make_async_copy(others, others, relay_send).wait()
        for copy in turns:
            copy.wait_send()
        send_halos()

        total = jnp.zeros((count, BLK), F32)
        size = tiles // WAVES
        for wave in range(WAVES):
            for part in range(3):
                got = received.at[part, wave * size : (wave + 1) * size]
                pltpu.make_async_copy(got, got, slot_recv.at[part, wave]).wait()
                lanes = slice(wave * size * SLOT, (wave + 1) * size * SLOT)
                total += jnp.dot(
                    spread[part, :, lanes],
                    received[part, wave * size : (wave + 1) * size].reshape(size * SLOT, BLK),
                    preferred_element_type=F32,
                )
        final[0:count, :] = final[0:count, :] + dt * total
        write_part(0)
        fix(0, 1)


def store(state, aux, state_out, aux_out, sem):
    copies = [
        pltpu.make_async_copy(a, b, sem.at[i])
        for i, (a, b) in enumerate(((state, state_out), (aux, aux_out)))
    ]
    for copy in copies:
        copy.start()
    for copy in copies:
        copy.wait()


def shards(tiles, fields, face_aux, block_owner):
    _, parts, rows, depth = fields.shape
    order = face_aux.shape[2]
    count = rows * depth // BLK
    span = rows + 2 * HALO
    vmem = pl.BlockSpec(memory_space=pltpu.VMEM)
    anywhere = pl.BlockSpec(memory_space=pltpu.HBM)
    dma = pltpu.SemaphoreType.DMA
    args = [
        pltpu.with_memory_space_constraint(a, pltpu.HBM) for a in (fields, face_aux, block_owner)
    ]
    results = pl.pallas_call(
        functools.partial(kernel, tiles),
        out_shape=(pltpu.VMEM(fields.shape, F32), pltpu.VMEM(face_aux.shape, F32)),
        in_specs=[anywhere] * 3,
        out_specs=(vmem, vmem),
        scratch_shapes=[
            pltpu.VMEM((parts, rows, depth), F32),
            pltpu.VMEM((parts * span * 8, BLK), F32),
            pltpu.VMEM((parts * span * 8, BLK), F32),
            pltpu.VMEM((parts * rows * 8, BLK), F32),
            pltpu.VMEM((1, count), jnp.int32),
            pltpu.VMEM((2, order, rows), F32),
            pltpu.VMEM((2, 2, order, rows), F32),
            pltpu.VMEM((2, parts * HALO * 8, BLK), BF16),
            pltpu.VMEM((2, parts * HALO * 8, BLK), BF16),
            pltpu.VMEM((tiles * SLOT, count), BF16),
            pltpu.VMEM((count, BLK), BF16),
            pltpu.VMEM((tiles, SLOT // 2, 2, BLK), BF16),
            pltpu.VMEM((tiles, 1, BLK), F32),
            pltpu.VMEM((3, tiles, 1, BLK), F32),
            pltpu.VMEM((tiles, 1, BLK), F32),
            pltpu.VMEM((3, tiles, SLOT // 2, 2, BLK), BF16),
            pltpu.VMEM((3, count, tiles * SLOT), BF16),
            dma((3,)), dma((2,)), dma((2,)), dma((2,)), dma((2,)), dma((2,)),
            dma, dma((3,)), dma, dma, dma, dma, dma((3, WAVES)),
            pltpu.SemaphoreType.REGULAR,
        ],
        compiler_params=pltpu.CompilerParams(
            collective_id=0, has_side_effects=True, vmem_limit_bytes=40 << 20
        ),
    )(*args)
    return pl.pallas_call(
        store,
        out_shape=(pltpu.HBM(fields.shape, F32), pltpu.HBM(face_aux.shape, F32)),
        in_specs=[vmem, vmem],
        out_specs=(anywhere, anywhere),
        scratch_shapes=[dma((2,))],
    )(*results)


def solution(mesh):
    return jax.shard_map(
        functools.partial(shards, mesh.shape["tile"]),
        mesh=mesh,
        in_specs=(P("grp", None, "tile", None), P("grp", None, None, "tile"), P("grp", "tile")),
        out_specs=(P("grp", None, "tile", None), P("grp", None, None, "tile")),
        check_vma=False,
    )
```

```python
import functools
import math

import jax
import jax.numpy as jnp
from jax import lax
from jax.experimental import pallas as pl
from jax.experimental.pallas import tpu as pltpu
from jax.sharding import PartitionSpec as P

MESH = pl.DeviceIdType.MESH


def ring(step):
    return min(step, 4 - step)


F32 = jnp.float32
BF16 = jnp.bfloat16

BLK = 128
SLOT = 12
LANES = 16
COLUMNS = sorted(range(16), key=lambda c: (-ring(c // 4) - ring(c % 4), c))
FAR_COLUMNS = sum(ring(c // 4) + ring(c % 4) > 2 for c in COLUMNS)
HALO = 4

LES_DT = 0.1
VISCOSITY = 1.0
ACOUSTIC_DT = 0.2
MACH = 0.3
TANGENT = 1.0
NEAR = 8.0 * LES_DT / 12.0
FAR = LES_DT / 12.0
DIFF = VISCOSITY * LES_DT


def iota(shape, dim):
    return lax.broadcasted_iota(jnp.int32, shape, dim)


def tile_at(tile, column, step):
    y, x, z = tile // 16, lax.rem(tile // 4, 4), lax.rem(tile, 4)
    y, x = lax.rem(y + column // 4, 4), lax.rem(x + column % 4, 4)
    z = (3 - z, 2 + lax.rem(z, 2) * 2 - z, 1 + z // 2 * 4 - z, z)[step]
    return y * 16 + x * 4 + z


def turn_of(target, tile):
    y, x, z = tile // 16, lax.rem(tile // 4, 4), lax.rem(tile, 4)
    dy = jnp.bitwise_and(lax.shift_right_logical(target, 4) - y, 3)
    dx = jnp.bitwise_and(lax.shift_right_logical(target, 2) - x, 3)
    dz = 3 - jnp.bitwise_xor(jnp.bitwise_and(target, 3), z)
    code = dy * 4 + dx
    place = jnp.zeros_like(code)
    for i, column in enumerate(COLUMNS):
        place = jnp.where(code == column, i, place)
    return place * 4 + dz


def exact_dot(a, b, dims):
    return lax.dot_general(
        a, b, (dims, ((), ())), precision=lax.Precision.HIGHEST, preferred_element_type=F32
    )


def roll(x, shift, axis):
    return pltpu.roll(x, shift % x.shape[axis], axis)


def ahead(one, two):
    lane, sub = iota((1, 8, BLK), 2), iota((1, 8, BLK), 1)
    one, two = roll(one, -1, 2), roll(two, -2, 2)
    own = jnp.where(lane < BLK - 1, one, 0.0) + jnp.where(lane < BLK - 2, two, 0.0)
    cross = jnp.where((lane == BLK - 1) & (sub > 0), one, 0.0) + jnp.where(
        (lane >= BLK - 2) & (sub > 0), two, 0.0
    )
    return own + roll(cross, -1, 1)


def behind(one, two):
    lane, sub = iota((1, 8, BLK), 2), iota((1, 8, BLK), 1)
    one, two = roll(one, 1, 2), roll(two, 2, 2)
    own = jnp.where(lane >= 1, one, 0.0) + jnp.where(lane >= 2, two, 0.0)
    cross = jnp.where((lane == 0) & (sub < 7), one, 0.0) + jnp.where(
        (lane < 2) & (sub < 7), two, 0.0
    )
    return own + roll(cross, 1, 1)


def rows_at(ref, part, row, count, span):
    start = pl.multiple_of((part * span + row) * 8, 8)
    return ref[pl.ds(start, count * 8), :].reshape(count, 8, BLK)


def put_rows(ref, part, row, value, span):
    start = pl.multiple_of((part * span + row) * 8, 8)
    ref[pl.ds(start, value.shape[0] * 8), :] = value.reshape(value.shape[0] * 8, BLK)


def les_rows(src, row, count, span):
    u = rows_at(src, 0, row - 2, count + 4, span)
    w = rows_at(src, 2, row, count, span)
    up, down, far = DIFF - NEAR * u[3:-1], DIFF + NEAR * u[1:-3], FAR * u
    right, left, side = DIFF - NEAR * w, DIFF + NEAR * w, FAR * w
    out = []
    for part in range(4):
        q = rows_at(src, part, row - 2, count + 4, span)
        core, bent = q[2:-2], far * q
        across = up * q[3:-1] + down * q[1:-3] + (bent[4:] - bent[:-4])
        edge = side * core
        along = ahead(right * core, edge) + behind(left * core, -edge)
        out.append((1.0 - 4.0 * DIFF) * core + across + along)
    return out


def source_rows(state):
    mix = state[0] * state[0] - state[2] * state[2] + state[1] * state[3]
    none = jnp.zeros_like(mix)
    quarter = 0.25 * mix
    return ahead(quarter, none) + behind(quarter, none) + 0.5 * mix


def slope_rows(q):
    return (q[:-4] - q[4:] + 8.0 * (q[3:-1] - q[1:-3])) * (1.0 / 12.0)


def slope_depth(q):
    near = (8.0 / 12.0) * q
    far = (1.0 / 12.0) * q
    return ahead(near, -far) + behind(-near, far)


def spread_rows(stage, state, first, count):
    span = state.shape[0] // 32
    for part in range(4):
        for lane in range(8):
            start = (part * span + HALO + first) * 8 + lane
            state[pl.ds(start, count, stride=8), :] = stage[
                part, first : first + count, lane * BLK : (lane + 1) * BLK
            ]


def write_part(final, out, part):
    rows = out.shape[2]
    for lane in range(8):
        out[0, part, :, lane * BLK : (lane + 1) * BLK] = final[
            pl.ds(part * rows * 8 + lane, rows, stride=8), :
        ]


class Halos:
    def __init__(self, tiles, tile, state, halo_out, halo_in, send, recv):
        self.state, self.halo_out, self.halo_in = state, halo_out, halo_in
        self.has_before, self.has_after = tile > 0, tile < tiles - 1
        wheres = (lax.rem(tile + tiles - 1, tiles), lax.rem(tile + 1, tiles))
        self.copies = [
            pltpu.make_async_remote_copy(
                halo_out.at[i], halo_in.at[i], send.at[i], recv.at[i],
                device_id={"tile": where}, device_id_type=MESH,
            )
            for i, where in enumerate(wheres)
        ]
        self.span = state.shape[0] // 32
        self.rows = self.span - 2 * HALO

    def pack(self):
        for part in range(4):
            piece = slice(part * HALO * 8, (part + 1) * HALO * 8)
            low = rows_at(self.state, part, HALO, HALO, self.span)
            high = rows_at(self.state, part, self.rows, HALO, self.span)
            self.halo_out[0, piece] = low.reshape(-1, BLK).astype(BF16)
            self.halo_out[1, piece] = high.reshape(-1, BLK).astype(BF16)

    def start(self):
        for copy, there in zip(self.copies, (self.has_before, self.has_after)):
            pl.when(there)(copy.start)

    def take(self):
        for copy, there in zip(self.copies, (self.has_after, self.has_before)):
            pl.when(there)(copy.wait_recv)
        for part in range(4):
            piece = slice(part * HALO * 8, (part + 1) * HALO * 8)
            upper = jnp.where(self.has_after, self.halo_in[0, piece].astype(F32), 0.0)
            lower = jnp.where(self.has_before, self.halo_in[1, piece].astype(F32), 0.0)
            put_rows(self.state, part, 0, lower.reshape(HALO, 8, BLK), self.span)
            put_rows(self.state, part, self.rows + HALO, upper.reshape(HALO, 8, BLK), self.span)

    def finish(self):
        for copy, there in zip(self.copies, (self.has_before, self.has_after)):
            pl.when(there)(copy.wait_send)


def row_loads(fields, stage, sem):
    rows = stage.shape[1]
    edges = (slice(0, 8), slice(rows - 8, rows), slice(8, rows - 8))
    return [
        pltpu.make_async_copy(fields.at[0, :, part], stage.at[:, part], sem.at[i])
        for i, part in enumerate(edges)
    ]


def les_kernel(
    tiles, fields, owner, final, packed, names,
    stage, state, middle, own, halo_out, halo_in, pack, blocks, ids,
    load_sem, own_sem, halo_send, halo_recv, id_send, id_recv,
):
    rows = stage.shape[1]
    span = rows + 2 * HALO
    group, tile = lax.axis_index("grp"), lax.axis_index("tile")
    last = lax.axis_size("grp") - 1
    halos = Halos(tiles, tile, state, halo_out, halo_in, halo_send, halo_recv)
    barrier = pltpu.get_barrier_semaphore()

    @pl.when(group < last)
    def _():
        loads = row_loads(fields, stage, load_sem)
        own_load = pltpu.make_async_copy(owner, own, own_sem)
        for copy in loads[:2]:
            copy.start()
        own_load.start()
        loads[2].start()

        @pl.when(group < 2)
        def _():
            pl.semaphore_signal(
                barrier, inc=1, device_id={"grp": lax.rem(group + 1, 2)}, device_id_type=MESH
            )

        for there, step in ((halos.has_before, tiles - 1), (halos.has_after, 1)):

            @pl.when(there)
            def _():
                pl.semaphore_signal(
                    barrier, inc=1, device_id={"tile": lax.rem(tile + step, tiles)},
                    device_id_type=MESH,
                )

        loads[0].wait()
        loads[1].wait()
        spread_rows(stage, state, 0, 8)
        spread_rows(stage, state, rows - 8, 8)
        halos.pack()
        paired = group < 2
        neighbours = halos.has_before.astype(jnp.int32) + halos.has_after.astype(jnp.int32)
        neighbours = neighbours + paired.astype(jnp.int32)
        id_copy = pltpu.make_async_remote_copy(
            ids.at[0], ids.at[1], id_send, id_recv,
            device_id={"grp": lax.rem(group + 1, 2)}, device_id_type=MESH,
        )
        chip = lax.rem(tile, 4)

        def meet():
            pl.semaphore_wait(barrier, neighbours)
            halos.start()

        pl.when(chip == 3)(meet)
        own_load.wait()
        count = own.shape[1]
        owned = own[...]
        live = owned >= 0
        target = lax.shift_right_logical(owned, int(math.log2(count)))
        place = jnp.bitwise_and(owned, count - 1)
        turn = turn_of(target, tile)
        hit = (iota((tiles, count), 0) == turn) & live
        hits = jnp.where(hit, 1.0, 0.0)
        earlier = jnp.where(iota((count, count), 0) < iota((count, count), 1), 1.0, 0.0)
        ranks = jnp.dot(hits.astype(BF16), earlier.astype(BF16), preferred_element_type=F32)
        rank = jnp.sum(hits * ranks, axis=0, keepdims=True).astype(jnp.int32)
        slot = jnp.where(live, turn * SLOT + rank, -1)
        pack[...] = jnp.where(iota((tiles * SLOT, count), 0) == slot, 1.0, 0.0).astype(BF16)
        listed = (iota((8, count), 0) == lax.shift_right_logical(turn, 3)) & live
        high = jnp.where(listed, lax.shift_right_logical(place, 4).astype(F32), 0.0)
        low = jnp.where(listed, (jnp.bitwise_and(place, 15) + 1).astype(F32), 0.0)
        lane = jnp.bitwise_and(turn, 7) * LANES + rank
        chosen = jnp.where(iota((BLK, count), 0) == lane, 1.0, 0.0).astype(BF16)
        digits = lax.dot_general(
            jnp.concatenate([high, low], axis=0).astype(BF16), chosen,
            (((1,), (1,)), ((), ())), preferred_element_type=F32,
        )
        ids[0] = 16.0 * digits[:8] + digits[8:]
        loads[2].wait()
        spread_rows(stage, state, 8, rows - 16)

        def first_step(row, size):
            for part, value in enumerate(les_rows(state, row, size, span)):
                put_rows(middle, part, row, value, span)

        def second_step(row, size):
            values = les_rows(middle, row, size, span)
            for part, value in enumerate(values):
                put_rows(final, part, row - HALO, value, rows)
            start = (row - HALO) * 8
            blocks[start : start + size * 8, :] = source_rows(values).reshape(-1, BLK).astype(BF16)

        first_step(6, rows - 4)
        pl.when((chip == 1) | (chip == 2))(meet)
        second_step(8, rows - 8)
        pl.when(chip == 0)(meet)
        pl.when(paired)(id_copy.start)
        pl.when(paired)(id_copy.wait_recv)
        turns, lane = iota((tiles, BLK), 0), iota((tiles, BLK), 1)
        chosen_row = jnp.where(iota((tiles, 8), 1) == iota((tiles, 8), 0) // 8, 1.0, 0.0)
        kept = lax.shift_right_logical(lane, 4) == jnp.bitwise_and(turns, 7)
        folded = jnp.bitwise_and(iota((BLK, BLK), 0), LANES - 1)

        def placed(listed, part):
            listed = jnp.where(kept, exact_dot(chosen_row, listed, ((1,), (0,))), 0.0)
            fold = jnp.where(iota((BLK, BLK), 1) == folded + part * LANES, 1.0, 0.0)
            return exact_dot(listed, fold, ((1,), (0,)))

        others = jnp.where(paired, ids[1], 0.0)
        listed = placed(ids[0], group) + placed(others, lax.rem(group + 1, 2))
        names[...] = listed.reshape(tiles, 1, BLK)

        halos.take()
        tops, bottoms = les_rows(state, 2, 4, span), les_rows(state, rows + 2, 4, span)
        for part in range(4):
            put_rows(middle, part, 2, tops[part], span)
            put_rows(middle, part, rows + 2, bottoms[part], span)
        for part in range(4):
            low_rows = rows_at(middle, part, 2, 2, span)
            put_rows(middle, part, 2, jnp.where(halos.has_before, low_rows, 0.0), span)
            high_rows = rows_at(middle, part, rows + 4, 2, span)
            put_rows(middle, part, rows + 4, jnp.where(halos.has_after, high_rows, 0.0), span)
        tops, bottoms = les_rows(middle, 4, 4, span), les_rows(middle, rows, 4, span)
        for values, row in ((tops, 0), (bottoms, rows - 4)):
            for part in range(4):
                put_rows(final, part, row, values[part], rows)
            start = row * 8
            blocks[start : start + 32, :] = source_rows(values).reshape(-1, BLK).astype(BF16)
        chosen_blocks = jnp.dot(pack[...], blocks[...], preferred_element_type=F32)
        packed[...] = chosen_blocks.astype(BF16).reshape(packed.shape)
        halos.finish()
        pl.when(paired)(id_copy.wait_send)


def exchange_kernel(
    tiles, fields, face_aux, les, packed, names, out, aux_out,
    stage, state, final, aux, aux_sides, halo_out, halo_in,
    names_in, received, spread,
    load_sem, aux_sem, halo_send, halo_recv, aux_send, aux_recv,
    name_send, name_recv, slot_send, slot_recv, partner_in,
):
    rows = stage.shape[1]
    span = rows + 2 * HALO
    group, tile = lax.axis_index("grp"), lax.axis_index("tile")
    last = lax.axis_size("grp") - 1
    after, before = lax.rem(tile + 1, tiles), lax.rem(tile + tiles - 1, tiles)
    halos = Halos(tiles, tile, state, halo_out, halo_in, halo_send, halo_recv)
    barrier = pltpu.get_barrier_semaphore()
    far = 4 * FAR_COLUMNS
    waves = [(0, far), (far, far + 24), (far + 24, tiles - 8), (tiles - 8, tiles)]

    half = tiles // 2

    def send(name_turns, order):
        def send_names(turn, which):
            pltpu.make_async_remote_copy(
                names.at[turn], names_in.at[which, turn], name_send, name_recv.at[which],
                device_id=there(COLUMNS[turn // 4], turn % 4), device_id_type=MESH,
            ).start()

        there = lambda c, k: {"grp": last, "tile": tile_at(tile, c, k)}
        which = 1 if len(name_turns) == tiles else 0
        for turn in name_turns:
            send_names(turn, which)
        for place, column in enumerate(COLUMNS):
            wave = sum(end <= 4 * place for _, end in waves)
            for step in order:
                turn = 4 * place + step
                pltpu.make_async_remote_copy(
                    packed.at[turn], received.at[group, turn], slot_send,
                    slot_recv.at[which, wave], device_id=there(column, step), device_id_type=MESH,
                ).start()

    def tell(sem, **there):
        pl.semaphore_signal(sem, inc=1, device_id=there, device_id_type=MESH)

    for mine, heard in ((0, far), (1, tiles - far)):

        @pl.when(group == mine)
        def _():
            tell(barrier, grp=1 - mine)
            pl.semaphore_wait(barrier, heard + 1)
            tell(partner_in, grp=1 - mine)
            pl.semaphore_wait(partner_in, 1)
            send(range(mine * half, (mine + 1) * half), (3, 2, 1, 0))
            sent = names.at[pl.ds(0, half)]
            pltpu.make_async_copy(sent, sent, name_send).wait()

    @pl.when(group == 2)
    def _():
        pl.semaphore_wait(barrier, tiles)
        send(range(tiles), range(4))
        pltpu.make_async_copy(names, names, name_send).wait()

    @pl.when(group < last)
    def _():
        for part in range(4):
            write_part(les, out, part)
        aux_load = pltpu.make_async_copy(face_aux.at[0], aux_out.at[0], aux_sem)
        aux_load.start()
        aux_load.wait()
        pltpu.make_async_copy(packed, packed, slot_send).wait()

    @pl.when(group == last)
    def _():
        for where in (before, after):
            pl.semaphore_signal(barrier, inc=1, device_id={"tile": where}, device_id_type=MESH)

        for place, column in enumerate(COLUMNS):

            for step in range(4):
                where = tile_at(tile, column, step)
                tell(barrier, grp=0 if place < FAR_COLUMNS else 1, tile=where)
                tell(barrier, grp=2, tile=where)

        loads = row_loads(fields, stage, load_sem)
        aux_load = pltpu.make_async_copy(face_aux.at[0], aux, aux_sem)
        for copy in loads:
            copy.start()
        aux_load.start()
        for copy in loads:
            copy.wait()
        spread_rows(stage, state, 0, rows)
        halos.pack()
        aux_load.wait()
        turns = [
            pltpu.make_async_remote_copy(
                aux, aux_sides.at[i], aux_send.at[i], aux_recv.at[i],
                device_id={"tile": where}, device_id_type=MESH,
            )
            for i, where in ((0, before), (1, after))
        ]
        pl.semaphore_wait(barrier, 2)
        halos.start()
        for copy in turns:
            copy.start()
        halos.take()

        dt = ACOUSTIC_DT

        size = rows // 4

        @pl.loop(0, 4)
        def _(step):
            row = HALO + step * size
            p, u, w, r = (rows_at(state, part, row - 2, size + 4, span) for part in range(4))
            dp, du, dw, dr = (slope_rows(q) for q in (p, u, w, r))
            p, u, w, r = (q[2:-2] for q in (p, u, w, r))
            div = du + slope_depth(w)
            news = (
                p + dt * (-MACH * dp - div),
                u + dt * (-MACH * du - dp),
                w + dt * (-MACH * dw - slope_depth(p)),
                r + dt * (-MACH * dr - div),
            )
            for part, value in enumerate(news):
                put_rows(final, part, step * size, value, rows)

        for copy in turns:
            copy.wait_recv()
        order = aux.shape[1]
        level = iota((order, 1), 0).astype(F32)
        rates = 0.1 * (level + 1.0)
        coupling = 0.5 + 0.5 * jnp.cos(math.pi * (level + 0.5) / order)
        here, there = iota((rows, rows), 0), iota((rows, rows), 1)
        bend = jnp.where(here == there, -2.0, 0.0) + jnp.where(
            (here == there + 1) | (here == there - 1), 1.0, 0.0
        )
        from_after = jnp.where((here == 0) & (there == rows - 1), 1.0, 0.0)
        from_before = jnp.where((here == rows - 1) & (there == 0), 1.0, 0.0)
        lane = iota((8, BLK), 1)
        kind = iota((8, BLK), 0)
        fixes = []
        for face in range(2):
            column = slice(0, BLK) if face == 0 else slice(7 * BLK, 8 * BLK)
            press, vel = stage[0, :, column], stage[2, :, column]
            mixed = 0.5 * (press - vel) if face == 0 else 0.5 * (press + vel)
            pick = jnp.where(lane == (0 if face == 0 else BLK - 1), 1.0, 0.0)
            outgoing = exact_dot(pick, mixed, ((1,), (1,)))[0:1]
            old = aux[face]
            second = (
                exact_dot(old, bend, ((1,), (0,)))
                + exact_dot(aux_sides[0, face], from_after, ((1,), (0,)))
                + exact_dot(aux_sides[1, face], from_before, ((1,), (0,)))
            )
            prior = jnp.concatenate([outgoing, old[:-1]], axis=0)
            new = old + dt * (-rates * old + coupling * (prior - old) + TANGENT * second)
            aux_out[0, face] = new
            incoming = jnp.sum(new, axis=0, keepdims=True) * (1.0 / order)
            ghost_p = outgoing + incoming
            ghost_w = incoming - outgoing if face == 0 else outgoing - incoming
            if face == 0:
                shape = jnp.where(lane == 0, -7.0 / 12.0, 0.0) + jnp.where(lane == 1, 1.0 / 12.0, 0.0)
            else:
                shape = jnp.where(lane == BLK - 1, 7.0 / 12.0, 0.0) + jnp.where(
                    lane == BLK - 2, -1.0 / 12.0, 0.0
                )
            shape = jnp.where(kind == 0, -dt * shape, 0.0)
            wide = [jnp.broadcast_to(g, (8, rows)) for g in (ghost_p, ghost_w)]
            fixes.append([exact_dot(g, shape, ((0,), (0,))) for g in wide])

        def fix(part, which):
            for face, column in ((0, slice(0, BLK)), (1, slice(7 * BLK, 8 * BLK))):
                out[0, part, :, column] = out[0, part, :, column] + fixes[face][which]

        for part in range(1, 4):
            write_part(final, out, part)
        fix(2, 0)
        fix(3, 1)

        for copy in turns:
            copy.wait_send()
        halos.finish()
        count, slots = spread.shape[1:]
        item = iota((1, slots), 1)
        item_turn = lax.shift_right_logical(item * 43691, 19)
        item_rank = item - item_turn * SLOT

        total = jnp.zeros((count, BLK), F32)

        def match(which):
            got = names_in.at[which]
            pltpu.make_async_copy(got, got, name_recv.at[which]).wait()
            listed = names_in[which].reshape(tiles, BLK)
            for part in ((0, 1), (2,))[which]:
                column = jnp.where(iota((BLK, slots), 0) == item_rank + part * LANES, 1.0, 0.0)
                item_name = exact_dot(listed, column, ((1,), (0,)))
                item_name = jnp.where(iota((tiles, slots), 0) == item_turn, item_name, 0.0)
                item_name = jnp.sum(item_name, axis=0, keepdims=True).astype(jnp.int32) - 1
                same = iota((count, slots), 0) == item_name
                spread[part] = jnp.where(same, 1.0, 0.0).astype(BF16)

        def collect(total, which, wave):
            first, end = waves[wave]
            parts = ((0, 1), (2,))[which]
            got = received.at[parts[0] : parts[-1] + 1, first:end]
            pltpu.make_async_copy(got, got, slot_recv.at[which, wave]).wait()
            for part in parts:
                total += jnp.dot(
                    spread[part, :, first * SLOT : end * SLOT],
                    received[part, first:end].reshape((end - first) * SLOT, BLK),
                    preferred_element_type=F32,
                )
            return total

        match(0)
        match(1)
        for wave in range(3):
            total = collect(total, 0, wave)
        for wave in range(3):
            total = collect(total, 1, wave)
        total = collect(total, 0, 3)
        total = collect(total, 1, 3)
        final[0:count, :] = final[0:count, :] + dt * total
        write_part(final, out, 0)
        fix(0, 1)


def store(state, aux, state_out, aux_out, sem):
    copies = [
        pltpu.make_async_copy(a, b, sem.at[i])
        for i, (a, b) in enumerate(((state, state_out), (aux, aux_out)))
    ]
    for copy in copies:
        copy.start()
    for copy in copies:
        copy.wait()


def shards(tiles, fields, face_aux, block_owner):
    _, parts, rows, depth = fields.shape
    order = face_aux.shape[2]
    count = rows * depth // BLK
    span = rows + 2 * HALO
    vmem = pl.BlockSpec(memory_space=pltpu.VMEM)
    hbm = pl.BlockSpec(memory_space=pltpu.HBM)
    dma = pltpu.SemaphoreType.DMA
    fields, face_aux, block_owner = (
        pltpu.with_memory_space_constraint(a, pltpu.HBM) for a in (fields, face_aux, block_owner)
    )
    in_vmem = lambda *arrays: [pltpu.with_memory_space_constraint(a, pltpu.VMEM) for a in arrays]
    stage = pltpu.VMEM((parts, rows, depth), F32)
    wide = pltpu.VMEM((parts * span * 8, BLK), F32)
    exact = pltpu.VMEM((parts * rows * 8, BLK), F32)
    halo = pltpu.VMEM((2, parts * HALO * 8, BLK), BF16)
    slots = (tiles, SLOT // 2, 2, BLK)
    names = (tiles, 1, BLK)
    les, packed, ids = pl.pallas_call(
        functools.partial(les_kernel, tiles),
        out_shape=(
            pltpu.VMEM((parts * rows * 8, BLK), F32), pltpu.VMEM(slots, BF16),
            pltpu.VMEM(names, F32),
        ),
        in_specs=[hbm, hbm],
        out_specs=(vmem, vmem, vmem),
        scratch_shapes=[
            stage, wide, wide, pltpu.VMEM((1, count), jnp.int32), halo, halo,
            pltpu.VMEM((tiles * SLOT, count), BF16), pltpu.VMEM((count, BLK), BF16),
            pltpu.VMEM((2, 8, BLK), F32), dma((3,)), dma, dma((2,)), dma((2,)), dma, dma,
        ],
        compiler_params=pltpu.CompilerParams(
            collective_id=0, has_side_effects=True, vmem_limit_bytes=40 << 20
        ),
    )(fields, block_owner)
    results = pl.pallas_call(
        functools.partial(exchange_kernel, tiles),
        out_shape=(pltpu.VMEM(fields.shape, F32), pltpu.VMEM(face_aux.shape, F32)),
        in_specs=[hbm, hbm, vmem, vmem, vmem],
        out_specs=(vmem, vmem),
        scratch_shapes=[
            stage, wide, exact, pltpu.VMEM((2, order, rows), F32),
            pltpu.VMEM((2, 2, order, rows), F32), halo, halo,
            pltpu.VMEM((2,) + names, F32),
            pltpu.VMEM((3,) + slots, BF16), pltpu.VMEM((3, count, tiles * SLOT), BF16),
            dma((3,)), dma, dma((2,)), dma((2,)), dma((2,)), dma((2,)),
            dma, dma((2,)), dma, dma((2, 4)),
            pltpu.SemaphoreType.REGULAR,
        ],
        compiler_params=pltpu.CompilerParams(
            collective_id=1, has_side_effects=True, vmem_limit_bytes=40 << 20
        ),
    )(fields, face_aux, *in_vmem(les, packed, ids))
    return pl.pallas_call(
        store,
        out_shape=(pltpu.HBM(fields.shape, F32), pltpu.HBM(face_aux.shape, F32)),
        in_specs=[vmem, vmem],
        out_specs=(hbm, hbm),
        scratch_shapes=[dma((2,))],
    )(*in_vmem(*results))


def solution(mesh):
    return jax.shard_map(
        functools.partial(shards, mesh.shape["tile"]),
        mesh=mesh,
        in_specs=(P("grp", None, "tile", None), P("grp", None, None, "tile"), P("grp", "tile")),
        out_specs=(P("grp", None, "tile", None), P("grp", None, None, "tile")),
        check_vma=False,
    )
```

```python
import functools
import math

import jax
import jax.numpy as jnp
from jax import lax
from jax.experimental import pallas as pl
from jax.experimental.pallas import tpu as pltpu
from jax.sharding import PartitionSpec as P

MESH = pl.DeviceIdType.MESH


def ring(step):
    return min(step, 4 - step)


F32 = jnp.float32
BF16 = jnp.bfloat16

BLK = 128
SLOT = 12
LANES = 16
COLUMNS = sorted(range(16), key=lambda c: (-ring(c // 4) - ring(c % 4), c))
FAR_COLUMNS = sum(ring(c // 4) + ring(c % 4) > 2 for c in COLUMNS)
HALO = 4

LES_DT = 0.1
VISCOSITY = 1.0
ACOUSTIC_DT = 0.2
MACH = 0.3
TANGENT = 1.0
NEAR = 8.0 * LES_DT / 12.0
FAR = LES_DT / 12.0
DIFF = VISCOSITY * LES_DT


def iota(shape, dim):
    return lax.broadcasted_iota(jnp.int32, shape, dim)


def tile_at(tile, column, step):
    y, x, z = tile // 16, lax.rem(tile // 4, 4), lax.rem(tile, 4)
    y, x = lax.rem(y + column // 4, 4), lax.rem(x + column % 4, 4)
    z = (3 - z, 2 + lax.rem(z, 2) * 2 - z, 1 + z // 2 * 4 - z, z)[step]
    return y * 16 + x * 4 + z


def turn_of(target, tile):
    y, x, z = tile // 16, lax.rem(tile // 4, 4), lax.rem(tile, 4)
    dy = jnp.bitwise_and(lax.shift_right_logical(target, 4) - y, 3)
    dx = jnp.bitwise_and(lax.shift_right_logical(target, 2) - x, 3)
    dz = 3 - jnp.bitwise_xor(jnp.bitwise_and(target, 3), z)
    code = dy * 4 + dx
    place = jnp.zeros_like(code)
    for i, column in enumerate(COLUMNS):
        place = jnp.where(code == column, i, place)
    return place * 4 + dz


def exact_dot(a, b, dims):
    return lax.dot_general(
        a, b, (dims, ((), ())), precision=lax.Precision.HIGHEST, preferred_element_type=F32
    )


def roll(x, shift, axis):
    return pltpu.roll(x, shift % x.shape[axis], axis)


def ahead(one, two):
    lane, sub = iota((1, 8, BLK), 2), iota((1, 8, BLK), 1)
    one, two = roll(one, -1, 2), roll(two, -2, 2)
    own = jnp.where(lane < BLK - 1, one, 0.0) + jnp.where(lane < BLK - 2, two, 0.0)
    cross = jnp.where((lane == BLK - 1) & (sub > 0), one, 0.0) + jnp.where(
        (lane >= BLK - 2) & (sub > 0), two, 0.0
    )
    return own + roll(cross, -1, 1)


def behind(one, two):
    lane, sub = iota((1, 8, BLK), 2), iota((1, 8, BLK), 1)
    one, two = roll(one, 1, 2), roll(two, 2, 2)
    own = jnp.where(lane >= 1, one, 0.0) + jnp.where(lane >= 2, two, 0.0)
    cross = jnp.where((lane == 0) & (sub < 7), one, 0.0) + jnp.where(
        (lane < 2) & (sub < 7), two, 0.0
    )
    return own + roll(cross, 1, 1)


def rows_at(ref, part, row, count, span):
    start = pl.multiple_of((part * span + row) * 8, 8)
    return ref[pl.ds(start, count * 8), :].reshape(count, 8, BLK)


def put_rows(ref, part, row, value, span):
    start = pl.multiple_of((part * span + row) * 8, 8)
    ref[pl.ds(start, value.shape[0] * 8), :] = value.reshape(value.shape[0] * 8, BLK)


def les_rows(src, row, count, span):
    u = rows_at(src, 0, row - 2, count + 4, span)
    w = rows_at(src, 2, row, count, span)
    up, down, far = DIFF - NEAR * u[3:-1], DIFF + NEAR * u[1:-3], FAR * u
    right, left, side = DIFF - NEAR * w, DIFF + NEAR * w, FAR * w
    out = []
    for part in range(4):
        q = rows_at(src, part, row - 2, count + 4, span)
        core, bent = q[2:-2], far * q
        across = up * q[3:-1] + down * q[1:-3] + (bent[4:] - bent[:-4])
        edge = side * core
        along = ahead(right * core, edge) + behind(left * core, -edge)
        out.append((1.0 - 4.0 * DIFF) * core + across + along)
    return out


def source_rows(state):
    mix = state[0] * state[0] - state[2] * state[2] + state[1] * state[3]
    none = jnp.zeros_like(mix)
    quarter = 0.25 * mix
    return ahead(quarter, none) + behind(quarter, none) + 0.5 * mix


def slope_rows(q):
    return (q[:-4] - q[4:] + 8.0 * (q[3:-1] - q[1:-3])) * (1.0 / 12.0)


def slope_depth(q):
    near = (8.0 / 12.0) * q
    far = (1.0 / 12.0) * q
    return ahead(near, -far) + behind(-near, far)


def spread_rows(stage, state, first, count):
    span = state.shape[0] // 32
    for part in range(4):
        for lane in range(8):
            start = (part * span + HALO + first) * 8 + lane
            state[pl.ds(start, count, stride=8), :] = stage[
                part, first : first + count, lane * BLK : (lane + 1) * BLK
            ]


def write_part(final, out, part):
    rows = out.shape[2]
    for lane in range(8):
        out[0, part, :, lane * BLK : (lane + 1) * BLK] = final[
            pl.ds(part * rows * 8 + lane, rows, stride=8), :
        ]


class Halos:
    def __init__(self, tiles, tile, state, halo_out, halo_in, send, recv):
        self.state, self.halo_out, self.halo_in = state, halo_out, halo_in
        self.has_before, self.has_after = tile > 0, tile < tiles - 1
        wheres = (lax.rem(tile + tiles - 1, tiles), lax.rem(tile + 1, tiles))
        self.copies = [
            pltpu.make_async_remote_copy(
                halo_out.at[i], halo_in.at[i], send.at[i], recv.at[i],
                device_id={"tile": where}, device_id_type=MESH,
            )
            for i, where in enumerate(wheres)
        ]
        self.span = state.shape[0] // 32
        self.rows = self.span - 2 * HALO

    def pack(self):
        for part in range(4):
            piece = slice(part * HALO * 8, (part + 1) * HALO * 8)
            low = rows_at(self.state, part, HALO, HALO, self.span)
            high = rows_at(self.state, part, self.rows, HALO, self.span)
            self.halo_out[0, piece] = low.reshape(-1, BLK).astype(BF16)
            self.halo_out[1, piece] = high.reshape(-1, BLK).astype(BF16)

    def start(self):
        for copy, there in zip(self.copies, (self.has_before, self.has_after)):
            pl.when(there)(copy.start)

    def take(self):
        for copy, there in zip(self.copies, (self.has_after, self.has_before)):
            pl.when(there)(copy.wait_recv)
        for part in range(4):
            piece = slice(part * HALO * 8, (part + 1) * HALO * 8)
            upper = jnp.where(self.has_after, self.halo_in[0, piece].astype(F32), 0.0)
            lower = jnp.where(self.has_before, self.halo_in[1, piece].astype(F32), 0.0)
            put_rows(self.state, part, 0, lower.reshape(HALO, 8, BLK), self.span)
            put_rows(self.state, part, self.rows + HALO, upper.reshape(HALO, 8, BLK), self.span)

    def finish(self):
        for copy, there in zip(self.copies, (self.has_before, self.has_after)):
            pl.when(there)(copy.wait_send)


def row_loads(fields, stage, sem):
    rows = stage.shape[1]
    edges = (slice(0, 8), slice(rows - 8, rows), slice(8, rows - 8))
    return [
        pltpu.make_async_copy(fields.at[0, :, part], stage.at[:, part], sem.at[i])
        for i, part in enumerate(edges)
    ]


def les_kernel(
    tiles, fields, owner, final, packed, names,
    stage, state, middle, own, halo_out, halo_in, pack, blocks, inner_slots, ids,
    load_sem, own_sem, halo_send, halo_recv, id_send, id_recv,
):
    rows = stage.shape[1]
    span = rows + 2 * HALO
    group, tile = lax.axis_index("grp"), lax.axis_index("tile")
    last = lax.axis_size("grp") - 1
    halos = Halos(tiles, tile, state, halo_out, halo_in, halo_send, halo_recv)
    barrier = pltpu.get_barrier_semaphore()

    @pl.when(group < last)
    def _():
        loads = row_loads(fields, stage, load_sem)
        own_load = pltpu.make_async_copy(owner, own, own_sem)
        for copy in loads[:2]:
            copy.start()
        own_load.start()
        loads[2].start()

        @pl.when(group < 2)
        def _():
            pl.semaphore_signal(
                barrier, inc=1, device_id={"grp": lax.rem(group + 1, 2)}, device_id_type=MESH
            )

        for there, step in ((halos.has_before, tiles - 1), (halos.has_after, 1)):

            @pl.when(there)
            def _():
                pl.semaphore_signal(
                    barrier, inc=1, device_id={"tile": lax.rem(tile + step, tiles)},
                    device_id_type=MESH,
                )

        loads[0].wait()
        loads[1].wait()
        spread_rows(stage, state, 0, 8)
        spread_rows(stage, state, rows - 8, 8)
        halos.pack()
        paired = group < 2
        neighbours = halos.has_before.astype(jnp.int32) + halos.has_after.astype(jnp.int32)
        neighbours = neighbours + paired.astype(jnp.int32)
        id_copy = pltpu.make_async_remote_copy(
            ids.at[0], ids.at[1], id_send, id_recv,
            device_id={"grp": lax.rem(group + 1, 2)}, device_id_type=MESH,
        )
        chip = lax.rem(tile, 4)

        def meet():
            pl.semaphore_wait(barrier, neighbours)
            halos.start()

        early, late = (group < 2) & (chip == 3), (group < 2) & (chip == 0)
        middling = (group == 2) & ((chip == 0) | (chip == 3))
        pl.when(early)(meet)
        own_load.wait()
        count = own.shape[1]
        owned = own[...]
        live = owned >= 0
        target = lax.shift_right_logical(owned, int(math.log2(count)))
        place = jnp.bitwise_and(owned, count - 1)
        turn = turn_of(target, tile)
        hit = (iota((tiles, count), 0) == turn) & live
        hits = jnp.where(hit, 1.0, 0.0)
        earlier = jnp.where(iota((count, count), 0) < iota((count, count), 1), 1.0, 0.0)
        ranks = jnp.dot(hits.astype(BF16), earlier.astype(BF16), preferred_element_type=F32)
        rank = jnp.sum(hits * ranks, axis=0, keepdims=True).astype(jnp.int32)
        slot = jnp.where(live, turn * SLOT + rank, -1)
        pack[...] = jnp.where(iota((tiles * SLOT, count), 0) == slot, 1.0, 0.0).astype(BF16)
        listed = (iota((8, count), 0) == lax.shift_right_logical(turn, 3)) & live
        high = jnp.where(listed, lax.shift_right_logical(place, 4).astype(F32), 0.0)
        low = jnp.where(listed, (jnp.bitwise_and(place, 15) + 1).astype(F32), 0.0)
        lane = jnp.bitwise_and(turn, 7) * LANES + rank
        chosen = jnp.where(iota((BLK, count), 0) == lane, 1.0, 0.0).astype(BF16)
        digits = lax.dot_general(
            jnp.concatenate([high, low], axis=0).astype(BF16), chosen,
            (((1,), (1,)), ((), ())), preferred_element_type=F32,
        )
        ids[0] = 16.0 * digits[:8] + digits[8:]
        loads[2].wait()
        spread_rows(stage, state, 8, rows - 16)

        def first_step(row, size):
            for part, value in enumerate(les_rows(state, row, size, span)):
                put_rows(middle, part, row, value, span)

        def second_step(row, size):
            values = les_rows(middle, row, size, span)
            for part, value in enumerate(values):
                put_rows(final, part, row - HALO, value, rows)
            start = (row - HALO) * 8
            blocks[start : start + size * 8, :] = source_rows(values).reshape(-1, BLK).astype(BF16)

        pl.when((chip == 1) | (chip == 2))(meet)
        first_step(6, rows - 4)
        pl.when(middling)(meet)
        second_step(8, rows - 8)
        pl.when(late)(meet)
        inner = slice(count // 4, 3 * count // 4)
        inner_slots[...] = jnp.dot(pack[:, inner], blocks[inner], preferred_element_type=F32)
        pl.when(paired)(id_copy.start)
        pl.when(paired)(id_copy.wait_recv)
        turns, lane = iota((tiles, BLK), 0), iota((tiles, BLK), 1)
        chosen_row = jnp.where(iota((tiles, 8), 1) == iota((tiles, 8), 0) // 8, 1.0, 0.0)
        kept = lax.shift_right_logical(lane, 4) == jnp.bitwise_and(turns, 7)
        folded = jnp.bitwise_and(iota((BLK, BLK), 0), LANES - 1)

        def placed(listed, part):
            listed = jnp.where(kept, exact_dot(chosen_row, listed, ((1,), (0,))), 0.0)
            fold = jnp.where(iota((BLK, BLK), 1) == folded + part * LANES, 1.0, 0.0)
            return exact_dot(listed, fold, ((1,), (0,)))

        others = jnp.where(paired, ids[1], 0.0)
        listed = placed(ids[0], group) + placed(others, lax.rem(group + 1, 2))
        names[...] = listed.reshape(tiles, 1, BLK)

        halos.take()
        tops, bottoms = les_rows(state, 2, 4, span), les_rows(state, rows + 2, 4, span)
        for part in range(4):
            put_rows(middle, part, 2, tops[part], span)
            put_rows(middle, part, rows + 2, bottoms[part], span)
        for part in range(4):
            low_rows = rows_at(middle, part, 2, 2, span)
            put_rows(middle, part, 2, jnp.where(halos.has_before, low_rows, 0.0), span)
            high_rows = rows_at(middle, part, rows + 4, 2, span)
            put_rows(middle, part, rows + 4, jnp.where(halos.has_after, high_rows, 0.0), span)
        tops, bottoms = les_rows(middle, 4, 4, span), les_rows(middle, rows, 4, span)
        for values, row in ((tops, 0), (bottoms, rows - 4)):
            for part in range(4):
                put_rows(final, part, row, values[part], rows)
            start = row * 8
            blocks[start : start + 32, :] = source_rows(values).reshape(-1, BLK).astype(BF16)
        chosen_blocks = inner_slots[...]
        for outer in (slice(0, count // 4), slice(3 * count // 4, count)):
            chosen_blocks += jnp.dot(pack[:, outer], blocks[outer], preferred_element_type=F32)
        packed[...] = chosen_blocks.astype(BF16).reshape(packed.shape)
        halos.finish()
        pl.when(paired)(id_copy.wait_send)


def exchange_kernel(
    tiles, fields, face_aux, les, packed, names, out, aux_out,
    stage, state, final, aux, aux_sides, halo_out, halo_in,
    names_in, received, spread,
    load_sem, aux_sem, halo_send, halo_recv, aux_send, aux_recv,
    name_send, name_recv, slot_send, slot_recv, partner_in,
):
    rows = stage.shape[1]
    span = rows + 2 * HALO
    group, tile = lax.axis_index("grp"), lax.axis_index("tile")
    last = lax.axis_size("grp") - 1
    after, before = lax.rem(tile + 1, tiles), lax.rem(tile + tiles - 1, tiles)
    halos = Halos(tiles, tile, state, halo_out, halo_in, halo_send, halo_recv)
    barrier = pltpu.get_barrier_semaphore()
    far = 4 * FAR_COLUMNS

    half = tiles // 2

    def send(name_turns, order):
        def send_names(turn, which):
            pltpu.make_async_remote_copy(
                names.at[turn], names_in.at[which, turn], name_send, name_recv.at[which],
                device_id=there(COLUMNS[turn // 4], turn % 4), device_id_type=MESH,
            ).start()

        there = lambda c, k: {"grp": last, "tile": tile_at(tile, c, k)}
        which = 1 if len(name_turns) == tiles else 0
        for turn in name_turns:
            send_names(turn, which)
        for place, column in enumerate(COLUMNS):
            for step in order:
                turn = 4 * place + step
                pltpu.make_async_remote_copy(
                    packed.at[turn], received.at[group, turn], slot_send,
                    slot_recv, device_id=there(column, step), device_id_type=MESH,
                ).start()

    def tell(sem, **there):
        pl.semaphore_signal(sem, inc=1, device_id=there, device_id_type=MESH)

    for mine, heard in ((0, far), (1, tiles - far)):

        @pl.when(group == mine)
        def _():
            tell(barrier, grp=1 - mine)
            pl.semaphore_wait(barrier, heard + 1)
            tell(partner_in, grp=1 - mine)
            pl.semaphore_wait(partner_in, 1)
            send(range(mine * half, (mine + 1) * half), (3, 2, 1, 0))
            sent = names.at[pl.ds(0, half)]
            pltpu.make_async_copy(sent, sent, name_send).wait()

    @pl.when(group == 2)
    def _():
        pl.semaphore_wait(barrier, tiles)
        send(range(tiles), range(4))
        pltpu.make_async_copy(names, names, name_send).wait()

    @pl.when(group < last)
    def _():
        for part in range(4):
            write_part(les, out, part)
        aux_load = pltpu.make_async_copy(face_aux.at[0], aux_out.at[0], aux_sem)
        aux_load.start()
        aux_load.wait()
        pltpu.make_async_copy(packed, packed, slot_send).wait()

    @pl.when(group == last)
    def _():
        for where in (before, after):
            pl.semaphore_signal(barrier, inc=1, device_id={"tile": where}, device_id_type=MESH)

        for place, column in enumerate(COLUMNS):

            for step in range(4):
                where = tile_at(tile, column, step)
                tell(barrier, grp=0 if place < FAR_COLUMNS else 1, tile=where)
                tell(barrier, grp=2, tile=where)

        loads = row_loads(fields, stage, load_sem)
        aux_load = pltpu.make_async_copy(face_aux.at[0], aux, aux_sem)
        for copy in loads:
            copy.start()
        aux_load.start()
        for copy in loads:
            copy.wait()
        spread_rows(stage, state, 0, rows)
        halos.pack()
        aux_load.wait()
        turns = [
            pltpu.make_async_remote_copy(
                aux, aux_sides.at[i], aux_send.at[i], aux_recv.at[i],
                device_id={"tile": where}, device_id_type=MESH,
            )
            for i, where in ((0, before), (1, after))
        ]
        pl.semaphore_wait(barrier, 2)
        halos.start()
        for copy in turns:
            copy.start()
        halos.take()

        dt = ACOUSTIC_DT

        size = rows // 4

        @pl.loop(0, 4)
        def _(step):
            row = HALO + step * size
            p, u, w, r = (rows_at(state, part, row - 2, size + 4, span) for part in range(4))
            dp, du, dw, dr = (slope_rows(q) for q in (p, u, w, r))
            p, u, w, r = (q[2:-2] for q in (p, u, w, r))
            div = du + slope_depth(w)
            news = (
                p + dt * (-MACH * dp - div),
                u + dt * (-MACH * du - dp),
                w + dt * (-MACH * dw - slope_depth(p)),
                r + dt * (-MACH * dr - div),
            )
            for part, value in enumerate(news):
                put_rows(final, part, step * size, value, rows)

        for copy in turns:
            copy.wait_recv()
        order = aux.shape[1]
        level = iota((order, 1), 0).astype(F32)
        rates = 0.1 * (level + 1.0)
        coupling = 0.5 + 0.5 * jnp.cos(math.pi * (level + 0.5) / order)
        here, there = iota((rows, rows), 0), iota((rows, rows), 1)
        bend = jnp.where(here == there, -2.0, 0.0) + jnp.where(
            (here == there + 1) | (here == there - 1), 1.0, 0.0
        )
        from_after = jnp.where((here == 0) & (there == rows - 1), 1.0, 0.0)
        from_before = jnp.where((here == rows - 1) & (there == 0), 1.0, 0.0)
        lane = iota((8, BLK), 1)
        kind = iota((8, BLK), 0)
        fixes = []
        for face in range(2):
            column = slice(0, BLK) if face == 0 else slice(7 * BLK, 8 * BLK)
            press, vel = stage[0, :, column], stage[2, :, column]
            mixed = 0.5 * (press - vel) if face == 0 else 0.5 * (press + vel)
            pick = jnp.where(lane == (0 if face == 0 else BLK - 1), 1.0, 0.0)
            outgoing = exact_dot(pick, mixed, ((1,), (1,)))[0:1]
            old = aux[face]
            second = (
                exact_dot(old, bend, ((1,), (0,)))
                + exact_dot(aux_sides[0, face], from_after, ((1,), (0,)))
                + exact_dot(aux_sides[1, face], from_before, ((1,), (0,)))
            )
            prior = jnp.concatenate([outgoing, old[:-1]], axis=0)
            new = old + dt * (-rates * old + coupling * (prior - old) + TANGENT * second)
            aux_out[0, face] = new
            incoming = jnp.sum(new, axis=0, keepdims=True) * (1.0 / order)
            ghost_p = outgoing + incoming
            ghost_w = incoming - outgoing if face == 0 else outgoing - incoming
            if face == 0:
                shape = jnp.where(lane == 0, -7.0 / 12.0, 0.0) + jnp.where(lane == 1, 1.0 / 12.0, 0.0)
            else:
                shape = jnp.where(lane == BLK - 1, 7.0 / 12.0, 0.0) + jnp.where(
                    lane == BLK - 2, -1.0 / 12.0, 0.0
                )
            shape = jnp.where(kind == 0, -dt * shape, 0.0)
            wide = [jnp.broadcast_to(g, (8, rows)) for g in (ghost_p, ghost_w)]
            fixes.append([exact_dot(g, shape, ((0,), (0,))) for g in wide])

        def fix(part, which):
            for face, column in ((0, slice(0, BLK)), (1, slice(7 * BLK, 8 * BLK))):
                out[0, part, :, column] = out[0, part, :, column] + fixes[face][which]

        for part in range(1, 4):
            write_part(final, out, part)
        fix(2, 0)
        fix(3, 1)

        for copy in turns:
            copy.wait_send()
        halos.finish()
        count, slots = spread.shape[1:]
        item = iota((1, slots), 1)
        item_turn = lax.shift_right_logical(item * 43691, 19)
        item_rank = item - item_turn * SLOT

        total = jnp.zeros((count, BLK), F32)

        def match(which):
            got = names_in.at[which]
            pltpu.make_async_copy(got, got, name_recv.at[which]).wait()
            listed = names_in[which].reshape(tiles, BLK)
            for part in ((0, 1), (2,))[which]:
                column = jnp.where(iota((BLK, slots), 0) == item_rank + part * LANES, 1.0, 0.0)
                item_name = exact_dot(listed, column, ((1,), (0,)))
                item_name = jnp.where(iota((tiles, slots), 0) == item_turn, item_name, 0.0)
                item_name = jnp.sum(item_name, axis=0, keepdims=True).astype(jnp.int32) - 1
                same = iota((count, slots), 0) == item_name
                spread[part] = jnp.where(same, 1.0, 0.0).astype(BF16)

        match(0)
        match(1)
        pltpu.make_async_copy(received, received, slot_recv).wait()
        for part in range(3):
            total += jnp.dot(spread[part], received[part].reshape(slots, BLK), preferred_element_type=F32)
        final[0:count, :] = final[0:count, :] + dt * total
        write_part(final, out, 0)
        fix(0, 1)


def store(state, aux, state_out, aux_out, sem):
    parts = state.shape[1]
    copies = [
        pltpu.make_async_copy(state.at[:, i], state_out.at[:, i], sem.at[i]) for i in range(parts)
    ]
    copies.append(pltpu.make_async_copy(aux, aux_out, sem.at[parts]))
    for copy in copies:
        copy.start()
    for copy in copies:
        copy.wait()


def shards(tiles, fields, face_aux, block_owner):
    _, parts, rows, depth = fields.shape
    order = face_aux.shape[2]
    count = rows * depth // BLK
    span = rows + 2 * HALO
    vmem = pl.BlockSpec(memory_space=pltpu.VMEM)
    hbm = pl.BlockSpec(memory_space=pltpu.HBM)
    dma = pltpu.SemaphoreType.DMA
    fields, face_aux, block_owner = (
        pltpu.with_memory_space_constraint(a, pltpu.HBM) for a in (fields, face_aux, block_owner)
    )
    in_vmem = lambda *arrays: [pltpu.with_memory_space_constraint(a, pltpu.VMEM) for a in arrays]
    stage = pltpu.VMEM((parts, rows, depth), F32)
    wide = pltpu.VMEM((parts * span * 8, BLK), F32)
    exact = pltpu.VMEM((parts * rows * 8, BLK), F32)
    halo = pltpu.VMEM((2, parts * HALO * 8, BLK), BF16)
    slots = (tiles, SLOT // 2, 2, BLK)
    names = (tiles, 1, BLK)
    les, packed, ids = pl.pallas_call(
        functools.partial(les_kernel, tiles),
        out_shape=(
            pltpu.VMEM((parts * rows * 8, BLK), F32), pltpu.VMEM(slots, BF16),
            pltpu.VMEM(names, F32),
        ),
        in_specs=[hbm, hbm],
        out_specs=(vmem, vmem, vmem),
        scratch_shapes=[
            stage, wide, wide, pltpu.VMEM((1, count), jnp.int32), halo, halo,
            pltpu.VMEM((tiles * SLOT, count), BF16), pltpu.VMEM((count, BLK), BF16),
            pltpu.VMEM((tiles * SLOT, BLK), F32), pltpu.VMEM((2, 8, BLK), F32), dma((3,)), dma, dma((2,)), dma((2,)), dma, dma,
        ],
        compiler_params=pltpu.CompilerParams(
            collective_id=0, has_side_effects=True, vmem_limit_bytes=40 << 20
        ),
    )(fields, block_owner)
    results = pl.pallas_call(
        functools.partial(exchange_kernel, tiles),
        out_shape=(pltpu.VMEM(fields.shape, F32), pltpu.VMEM(face_aux.shape, F32)),
        in_specs=[hbm, hbm, vmem, vmem, vmem],
        out_specs=(vmem, vmem),
        scratch_shapes=[
            stage, wide, exact, pltpu.VMEM((2, order, rows), F32),
            pltpu.VMEM((2, 2, order, rows), F32), halo, halo,
            pltpu.VMEM((2,) + names, F32),
            pltpu.VMEM((3,) + slots, BF16), pltpu.VMEM((3, count, tiles * SLOT), BF16),
            dma((3,)), dma, dma((2,)), dma((2,)), dma((2,)), dma((2,)),
            dma, dma((2,)), dma, dma,
            pltpu.SemaphoreType.REGULAR,
        ],
        compiler_params=pltpu.CompilerParams(
            collective_id=1, has_side_effects=True, vmem_limit_bytes=40 << 20
        ),
    )(fields, face_aux, *in_vmem(les, packed, ids))
    return pl.pallas_call(
        store,
        out_shape=(pltpu.HBM(fields.shape, F32), pltpu.HBM(face_aux.shape, F32)),
        in_specs=[vmem, vmem],
        out_specs=(hbm, hbm),
        scratch_shapes=[dma((parts + 1,))],
    )(*in_vmem(*results))


def solution(mesh):
    return jax.shard_map(
        functools.partial(shards, mesh.shape["tile"]),
        mesh=mesh,
        in_specs=(P("grp", None, "tile", None), P("grp", None, None, "tile"), P("grp", "tile")),
        out_specs=(P("grp", None, "tile", None), P("grp", None, None, "tile")),
        check_vma=False,
    )
```

```python
import functools
import math

import jax
import jax.numpy as jnp
from jax import lax
from jax.experimental import pallas as pl
from jax.experimental.pallas import tpu as pltpu
from jax.sharding import PartitionSpec as P

MESH = pl.DeviceIdType.MESH


def ring(step):
    return min(step, 4 - step)


F32 = jnp.float32
BF16 = jnp.bfloat16

BLK = 128
SLOT = 12
LANES = 16
WIDE = 2 * LANES
COLUMNS = sorted(range(16), key=lambda c: (-ring(c // 4) - ring(c % 4), c))
FAR_COLUMNS = sum(ring(c // 4) + ring(c % 4) > 2 for c in COLUMNS)
HALO = 4

LES_DT = 0.1
VISCOSITY = 1.0
ACOUSTIC_DT = 0.2
MACH = 0.3
TANGENT = 1.0
NEAR = 8.0 * LES_DT / 12.0
FAR = LES_DT / 12.0
DIFF = VISCOSITY * LES_DT


def iota(shape, dim):
    return lax.broadcasted_iota(jnp.int32, shape, dim)


def tile_at(tile, column, step):
    y, x, z = tile // 16, lax.rem(tile // 4, 4), lax.rem(tile, 4)
    y, x = lax.rem(y + column // 4, 4), lax.rem(x + column % 4, 4)
    z = (3 - z, 2 + lax.rem(z, 2) * 2 - z, 1 + z // 2 * 4 - z, z)[step]
    return y * 16 + x * 4 + z


def turn_of(target, tile):
    y, x, z = tile // 16, lax.rem(tile // 4, 4), lax.rem(tile, 4)
    dy = jnp.bitwise_and(lax.shift_right_logical(target, 4) - y, 3)
    dx = jnp.bitwise_and(lax.shift_right_logical(target, 2) - x, 3)
    dz = 3 - jnp.bitwise_xor(jnp.bitwise_and(target, 3), z)
    code = dy * 4 + dx
    place = jnp.zeros_like(code)
    for i, column in enumerate(COLUMNS):
        place = jnp.where(code == column, i, place)
    return place * 4 + dz


def exact_dot(a, b, dims):
    return lax.dot_general(
        a, b, (dims, ((), ())), precision=lax.Precision.HIGHEST, preferred_element_type=F32
    )


def roll(x, shift, axis):
    return pltpu.roll(x, shift % x.shape[axis], axis)


def ahead(one, two):
    lane, sub = iota((1, 8, BLK), 2), iota((1, 8, BLK), 1)
    one, two = roll(one, -1, 2), roll(two, -2, 2)
    own = jnp.where(lane < BLK - 1, one, 0.0) + jnp.where(lane < BLK - 2, two, 0.0)
    cross = jnp.where((lane == BLK - 1) & (sub > 0), one, 0.0) + jnp.where(
        (lane >= BLK - 2) & (sub > 0), two, 0.0
    )
    return own + roll(cross, -1, 1)


def behind(one, two):
    lane, sub = iota((1, 8, BLK), 2), iota((1, 8, BLK), 1)
    one, two = roll(one, 1, 2), roll(two, 2, 2)
    own = jnp.where(lane >= 1, one, 0.0) + jnp.where(lane >= 2, two, 0.0)
    cross = jnp.where((lane == 0) & (sub < 7), one, 0.0) + jnp.where(
        (lane < 2) & (sub < 7), two, 0.0
    )
    return own + roll(cross, 1, 1)


def rows_at(ref, part, row, count, span):
    start = pl.multiple_of((part * span + row) * 8, 8)
    return ref[pl.ds(start, count * 8), :].reshape(count, 8, BLK)


def put_rows(ref, part, row, value, span):
    start = pl.multiple_of((part * span + row) * 8, 8)
    ref[pl.ds(start, value.shape[0] * 8), :] = value.reshape(value.shape[0] * 8, BLK)


def les_rows(src, row, count, span):
    u = rows_at(src, 0, row - 2, count + 4, span)
    w = rows_at(src, 2, row, count, span)
    up, down, far = DIFF - NEAR * u[3:-1], DIFF + NEAR * u[1:-3], FAR * u
    right, left, side = DIFF - NEAR * w, DIFF + NEAR * w, FAR * w
    out = []
    for part in range(4):
        q = rows_at(src, part, row - 2, count + 4, span)
        core, bent = q[2:-2], far * q
        across = up * q[3:-1] + down * q[1:-3] + (bent[4:] - bent[:-4])
        edge = side * core
        along = ahead(right * core, edge) + behind(left * core, -edge)
        out.append((1.0 - 4.0 * DIFF) * core + across + along)
    return out


def source_rows(state):
    mix = state[0] * state[0] - state[2] * state[2] + state[1] * state[3]
    none = jnp.zeros_like(mix)
    quarter = 0.25 * mix
    return ahead(quarter, none) + behind(quarter, none) + 0.5 * mix


def slope_rows(q):
    return (q[:-4] - q[4:] + 8.0 * (q[3:-1] - q[1:-3])) * (1.0 / 12.0)


def slope_depth(q):
    near = (8.0 / 12.0) * q
    far = (1.0 / 12.0) * q
    return ahead(near, -far) + behind(-near, far)


def spread_rows(stage, state, first, count):
    span = state.shape[0] // 32
    for part in range(4):
        for lane in range(8):
            start = (part * span + HALO + first) * 8 + lane
            state[pl.ds(start, count, stride=8), :] = stage[
                part, first : first + count, lane * BLK : (lane + 1) * BLK
            ]


def write_part(final, out, part):
    rows = out.shape[2]
    for lane in range(8):
        out[0, part, :, lane * BLK : (lane + 1) * BLK] = final[
            pl.ds(part * rows * 8 + lane, rows, stride=8), :
        ]


class Halos:
    def __init__(self, tiles, tile, state, halo_out, halo_in, send, recv):
        self.state, self.halo_out, self.halo_in = state, halo_out, halo_in
        self.has_before, self.has_after = tile > 0, tile < tiles - 1
        wheres = (lax.rem(tile + tiles - 1, tiles), lax.rem(tile + 1, tiles))
        self.copies = [
            pltpu.make_async_remote_copy(
                halo_out.at[i], halo_in.at[i], send.at[i], recv.at[i],
                device_id={"tile": where}, device_id_type=MESH,
            )
            for i, where in enumerate(wheres)
        ]
        self.span = state.shape[0] // 32
        self.rows = self.span - 2 * HALO

    def pack(self):
        for part in range(4):
            piece = slice(part * HALO * 8, (part + 1) * HALO * 8)
            low = rows_at(self.state, part, HALO, HALO, self.span)
            high = rows_at(self.state, part, self.rows, HALO, self.span)
            self.halo_out[0, piece] = low.reshape(-1, BLK).astype(BF16)
            self.halo_out[1, piece] = high.reshape(-1, BLK).astype(BF16)

    def start(self):
        for copy, there in zip(self.copies, (self.has_before, self.has_after)):
            pl.when(there)(copy.start)

    def take(self):
        for copy, there in zip(self.copies, (self.has_after, self.has_before)):
            pl.when(there)(copy.wait_recv)
        for part in range(4):
            piece = slice(part * HALO * 8, (part + 1) * HALO * 8)
            upper = jnp.where(self.has_after, self.halo_in[0, piece].astype(F32), 0.0)
            lower = jnp.where(self.has_before, self.halo_in[1, piece].astype(F32), 0.0)
            put_rows(self.state, part, 0, lower.reshape(HALO, 8, BLK), self.span)
            put_rows(self.state, part, self.rows + HALO, upper.reshape(HALO, 8, BLK), self.span)

    def finish(self):
        for copy, there in zip(self.copies, (self.has_before, self.has_after)):
            pl.when(there)(copy.wait_send)


def row_loads(fields, stage, sem):
    rows = stage.shape[1]
    edges = (slice(0, 8), slice(rows - 8, rows), slice(8, rows - 8))
    return [
        pltpu.make_async_copy(fields.at[0, :, part], stage.at[:, part], sem.at[i])
        for i, part in enumerate(edges)
    ]


def les_kernel(
    tiles, fields, owner, final, packed, names,
    stage, state, middle, own, halo_out, halo_in, pack, blocks, inner_slots, ids,
    load_sem, own_sem, halo_send, halo_recv, id_send, id_recv,
):
    rows = stage.shape[1]
    span = rows + 2 * HALO
    group, tile = lax.axis_index("grp"), lax.axis_index("tile")
    last = lax.axis_size("grp") - 1
    halos = Halos(tiles, tile, state, halo_out, halo_in, halo_send, halo_recv)
    barrier = pltpu.get_barrier_semaphore()

    @pl.when(group < last)
    def _():
        loads = row_loads(fields, stage, load_sem)
        own_load = pltpu.make_async_copy(owner, own, own_sem)
        for copy in loads[:2]:
            copy.start()
        own_load.start()
        loads[2].start()

        @pl.when(group < 2)
        def _():
            pl.semaphore_signal(
                barrier, inc=1, device_id={"grp": lax.rem(group + 1, 2)}, device_id_type=MESH
            )

        for there, step in ((halos.has_before, tiles - 1), (halos.has_after, 1)):

            @pl.when(there)
            def _():
                pl.semaphore_signal(
                    barrier, inc=1, device_id={"tile": lax.rem(tile + step, tiles)},
                    device_id_type=MESH,
                )

        loads[0].wait()
        loads[1].wait()
        spread_rows(stage, state, 0, 8)
        spread_rows(stage, state, rows - 8, 8)
        halos.pack()
        paired = group < 2
        neighbours = halos.has_before.astype(jnp.int32) + halos.has_after.astype(jnp.int32)
        neighbours = neighbours + paired.astype(jnp.int32)
        id_copy = pltpu.make_async_remote_copy(
            ids.at[0], ids.at[1], id_send, id_recv,
            device_id={"grp": lax.rem(group + 1, 2)}, device_id_type=MESH,
        )
        chip = lax.rem(tile, 4)

        def meet():
            pl.semaphore_wait(barrier, neighbours)
            halos.start()

        early, late = (group < 2) & (chip == 3), (group < 2) & (chip == 0)
        middling = (group == 2) & ((chip == 0) | (chip == 3))
        pl.when(early)(meet)
        own_load.wait()
        count = own.shape[1]
        owned = own[...]
        live = owned >= 0
        target = lax.shift_right_logical(owned, int(math.log2(count)))
        place = jnp.bitwise_and(owned, count - 1)
        turn = turn_of(target, tile)
        hit = (iota((tiles, count), 0) == turn) & live
        hits = jnp.where(hit, 1.0, 0.0)
        earlier = jnp.where(iota((count, count), 0) < iota((count, count), 1), 1.0, 0.0)
        ranks = jnp.dot(hits.astype(BF16), earlier.astype(BF16), preferred_element_type=F32)
        rank = jnp.sum(hits * ranks, axis=0, keepdims=True).astype(jnp.int32)
        slot = jnp.where(live, turn * SLOT + rank, -1)
        pack[...] = jnp.where(iota((tiles * SLOT, count), 0) == slot, 1.0, 0.0).astype(BF16)
        listed = (iota((8, count), 0) == lax.shift_right_logical(turn, 3)) & live
        high = jnp.where(listed, lax.shift_right_logical(place, 4).astype(F32), 0.0)
        low = jnp.where(listed, (jnp.bitwise_and(place, 15) + 1).astype(F32), 0.0)
        lane = jnp.bitwise_and(turn, 7) * LANES + rank
        chosen = jnp.where(iota((BLK, count), 0) == lane, 1.0, 0.0).astype(BF16)
        digits = lax.dot_general(
            jnp.concatenate([high, low], axis=0).astype(BF16), chosen,
            (((1,), (1,)), ((), ())), preferred_element_type=F32,
        )
        ids[0] = 16.0 * digits[:8] + digits[8:]
        loads[2].wait()
        spread_rows(stage, state, 8, rows - 16)

        def first_step(row, size):
            for part, value in enumerate(les_rows(state, row, size, span)):
                put_rows(middle, part, row, value, span)

        def second_step(row, size):
            values = les_rows(middle, row, size, span)
            for part, value in enumerate(values):
                put_rows(final, part, row - HALO, value, rows)
            start = (row - HALO) * 8
            blocks[start : start + size * 8, :] = source_rows(values).reshape(-1, BLK).astype(BF16)

        pl.when((chip == 1) | (chip == 2))(meet)
        first_step(6, rows - 4)
        pl.when(middling)(meet)
        second_step(8, rows - 8)
        pl.when(late)(meet)
        inner = slice(count // 4, 3 * count // 4)
        inner_slots[...] = jnp.dot(pack[:, inner], blocks[inner], preferred_element_type=F32)
        pl.when(paired)(id_copy.start)
        pl.when(paired)(id_copy.wait_recv)
        turns, lane = iota((tiles, BLK), 0), iota((tiles, BLK), 1)
        chosen_row = jnp.where(iota((tiles, 8), 1) == iota((tiles, 8), 0) // 8, 1.0, 0.0)
        kept = lax.shift_right_logical(lane, 4) == jnp.bitwise_and(turns, 7)
        folded = jnp.bitwise_and(iota((BLK, WIDE), 0), LANES - 1)

        def placed(listed, part):
            listed = jnp.where(kept, exact_dot(chosen_row, listed, ((1,), (0,))), 0.0)
            fold = jnp.where(iota((BLK, WIDE), 1) == folded + part * LANES, 1.0, 0.0)
            return exact_dot(listed, fold, ((1,), (0,)))

        others = jnp.where(paired, ids[1], 0.0)
        listed = placed(ids[0], lax.rem(group, 2)) + placed(others, lax.rem(group + 1, 2))
        names[...] = listed.reshape(tiles, 1, WIDE)

        halos.take()
        tops, bottoms = les_rows(state, 2, 4, span), les_rows(state, rows + 2, 4, span)
        for part in range(4):
            put_rows(middle, part, 2, tops[part], span)
            put_rows(middle, part, rows + 2, bottoms[part], span)
        for part in range(4):
            low_rows = rows_at(middle, part, 2, 2, span)
            put_rows(middle, part, 2, jnp.where(halos.has_before, low_rows, 0.0), span)
            high_rows = rows_at(middle, part, rows + 4, 2, span)
            put_rows(middle, part, rows + 4, jnp.where(halos.has_after, high_rows, 0.0), span)
        tops, bottoms = les_rows(middle, 4, 4, span), les_rows(middle, rows, 4, span)
        for values, row in ((tops, 0), (bottoms, rows - 4)):
            for part in range(4):
                put_rows(final, part, row, values[part], rows)
            start = row * 8
            blocks[start : start + 32, :] = source_rows(values).reshape(-1, BLK).astype(BF16)
        chosen_blocks = inner_slots[...]
        for outer in (slice(0, count // 4), slice(3 * count // 4, count)):
            chosen_blocks += jnp.dot(pack[:, outer], blocks[outer], preferred_element_type=F32)
        packed[...] = chosen_blocks.astype(BF16).reshape(packed.shape)
        halos.finish()
        pl.when(paired)(id_copy.wait_send)


def exchange_kernel(
    tiles, fields, face_aux, les, packed, names, out, aux_out,
    stage, state, final, aux, aux_sides, halo_out, halo_in,
    names_in, received, spread,
    load_sem, aux_sem, halo_send, halo_recv, aux_send, aux_recv,
    name_send, name_recv, slot_send, slot_recv, partner_in,
):
    rows = stage.shape[1]
    span = rows + 2 * HALO
    group, tile = lax.axis_index("grp"), lax.axis_index("tile")
    last = lax.axis_size("grp") - 1
    after, before = lax.rem(tile + 1, tiles), lax.rem(tile + tiles - 1, tiles)
    halos = Halos(tiles, tile, state, halo_out, halo_in, halo_send, halo_recv)
    barrier = pltpu.get_barrier_semaphore()
    far = 4 * FAR_COLUMNS

    half = tiles // 2

    def send(name_turns, order):
        def send_names(turn, which):
            pltpu.make_async_remote_copy(
                names.at[turn], names_in.at[which, turn], name_send, name_recv.at[which],
                device_id=there(COLUMNS[turn // 4], turn % 4), device_id_type=MESH,
            ).start()

        there = lambda c, k: {"grp": last, "tile": tile_at(tile, c, k)}
        which = 1 if len(name_turns) == tiles else 0
        for turn in name_turns:
            send_names(turn, which)
        for place, column in enumerate(COLUMNS):
            for step in order:
                turn = 4 * place + step
                pltpu.make_async_remote_copy(
                    packed.at[turn], received.at[group, turn], slot_send,
                    slot_recv, device_id=there(column, step), device_id_type=MESH,
                ).start()

    def tell(sem, **there):
        pl.semaphore_signal(sem, inc=1, device_id=there, device_id_type=MESH)

    for mine, heard in ((0, far), (1, tiles - far)):

        @pl.when(group == mine)
        def _():
            tell(barrier, grp=1 - mine)
            pl.semaphore_wait(barrier, heard + 1)
            tell(partner_in, grp=1 - mine)
            pl.semaphore_wait(partner_in, 1)
            if mine == 0:
                pl.when(tile == 0)(lambda: pl.semaphore_wait(partner_in, 1))
            send(range(mine * half, (mine + 1) * half), (2, 1, 3, 0))
            if mine == 1:
                pl.when(tile == 0)(lambda: tell(partner_in, grp=0))
            sent = names.at[pl.ds(0, half)]
            pltpu.make_async_copy(sent, sent, name_send).wait()

    @pl.when(group == 2)
    def _():
        pl.semaphore_wait(barrier, tiles)
        send(range(tiles), range(4))
        pltpu.make_async_copy(names, names, name_send).wait()

    @pl.when(group < last)
    def _():
        for part in range(4):
            write_part(les, out, part)
        aux_load = pltpu.make_async_copy(face_aux.at[0], aux_out.at[0], aux_sem)
        aux_load.start()
        aux_load.wait()
        pltpu.make_async_copy(packed, packed, slot_send).wait()

    @pl.when(group == last)
    def _():
        for where in (before, after):
            pl.semaphore_signal(barrier, inc=1, device_id={"tile": where}, device_id_type=MESH)

        for place, column in enumerate(COLUMNS):

            for step in range(4):
                where = tile_at(tile, column, step)
                tell(barrier, grp=0 if place < FAR_COLUMNS else 1, tile=where)

        for place, column in enumerate(COLUMNS):
            for step in range(4):
                tell(barrier, grp=2, tile=tile_at(tile, column, step))

        loads = row_loads(fields, stage, load_sem)
        aux_load = pltpu.make_async_copy(face_aux.at[0], aux, aux_sem)
        for copy in loads:
            copy.start()
        aux_load.start()
        for copy in loads:
            copy.wait()
        spread_rows(stage, state, 0, rows)
        halos.pack()
        aux_load.wait()
        turns = [
            pltpu.make_async_remote_copy(
                aux, aux_sides.at[i], aux_send.at[i], aux_recv.at[i],
                device_id={"tile": where}, device_id_type=MESH,
            )
            for i, where in ((0, before), (1, after))
        ]
        pl.semaphore_wait(barrier, 2)
        halos.start()
        for copy in turns:
            copy.start()
        halos.take()

        dt = ACOUSTIC_DT

        size = rows // 4

        @pl.loop(0, 4)
        def _(step):
            row = HALO + step * size
            p, u, w, r = (rows_at(state, part, row - 2, size + 4, span) for part in range(4))
            dp, du, dw, dr = (slope_rows(q) for q in (p, u, w, r))
            p, u, w, r = (q[2:-2] for q in (p, u, w, r))
            div = du + slope_depth(w)
            news = (
                p + dt * (-MACH * dp - div),
                u + dt * (-MACH * du - dp),
                w + dt * (-MACH * dw - slope_depth(p)),
                r + dt * (-MACH * dr - div),
            )
            for part, value in enumerate(news):
                put_rows(final, part, step * size, value, rows)

        for copy in turns:
            copy.wait_recv()
        order = aux.shape[1]
        level = iota((order, 1), 0).astype(F32)
        rates = 0.1 * (level + 1.0)
        coupling = 0.5 + 0.5 * jnp.cos(math.pi * (level + 0.5) / order)
        here, there = iota((rows, rows), 0), iota((rows, rows), 1)
        bend = jnp.where(here == there, -2.0, 0.0) + jnp.where(
            (here == there + 1) | (here == there - 1), 1.0, 0.0
        )
        from_after = jnp.where((here == 0) & (there == rows - 1), 1.0, 0.0)
        from_before = jnp.where((here == rows - 1) & (there == 0), 1.0, 0.0)
        lane = iota((8, BLK), 1)
        kind = iota((8, BLK), 0)
        fixes = []
        for face in range(2):
            column = slice(0, BLK) if face == 0 else slice(7 * BLK, 8 * BLK)
            press, vel = stage[0, :, column], stage[2, :, column]
            mixed = 0.5 * (press - vel) if face == 0 else 0.5 * (press + vel)
            pick = jnp.where(lane == (0 if face == 0 else BLK - 1), 1.0, 0.0)
            outgoing = exact_dot(pick, mixed, ((1,), (1,)))[0:1]
            old = aux[face]
            second = (
                exact_dot(old, bend, ((1,), (0,)))
                + exact_dot(aux_sides[0, face], from_after, ((1,), (0,)))
                + exact_dot(aux_sides[1, face], from_before, ((1,), (0,)))
            )
            prior = jnp.concatenate([outgoing, old[:-1]], axis=0)
            new = old + dt * (-rates * old + coupling * (prior - old) + TANGENT * second)
            aux_out[0, face] = new
            incoming = jnp.sum(new, axis=0, keepdims=True) * (1.0 / order)
            ghost_p = outgoing + incoming
            ghost_w = incoming - outgoing if face == 0 else outgoing - incoming
            if face == 0:
                shape = jnp.where(lane == 0, -7.0 / 12.0, 0.0) + jnp.where(lane == 1, 1.0 / 12.0, 0.0)
            else:
                shape = jnp.where(lane == BLK - 1, 7.0 / 12.0, 0.0) + jnp.where(
                    lane == BLK - 2, -1.0 / 12.0, 0.0
                )
            shape = jnp.where(kind == 0, -dt * shape, 0.0)
            wide = [jnp.broadcast_to(g, (8, rows)) for g in (ghost_p, ghost_w)]
            fixes.append([exact_dot(g, shape, ((0,), (0,))) for g in wide])

        def fix(part, which):
            for face, column in ((0, slice(0, BLK)), (1, slice(7 * BLK, 8 * BLK))):
                out[0, part, :, column] = out[0, part, :, column] + fixes[face][which]

        for part in range(1, 4):
            write_part(final, out, part)
        fix(2, 0)
        fix(3, 1)

        for copy in turns:
            copy.wait_send()
        halos.finish()
        count, slots = spread.shape[1:]
        item = iota((1, slots), 1)
        item_turn = lax.shift_right_logical(item * 43691, 19)
        item_rank = item - item_turn * SLOT

        total = jnp.zeros((count, BLK), F32)

        def match(which):
            got = names_in.at[which]
            pltpu.make_async_copy(got, got, name_recv.at[which]).wait()
            listed = names_in[which].reshape(tiles, WIDE)
            for part in ((0, 1), (2,))[which]:
                lane = item_rank + part % 2 * LANES
                column = jnp.where(iota((WIDE, slots), 0) == lane, 1.0, 0.0)
                item_name = exact_dot(listed, column, ((1,), (0,)))
                item_name = jnp.where(iota((tiles, slots), 0) == item_turn, item_name, 0.0)
                item_name = jnp.sum(item_name, axis=0, keepdims=True).astype(jnp.int32) - 1
                same = iota((count, slots), 0) == item_name
                spread[part] = jnp.where(same, 1.0, 0.0).astype(BF16)

        match(0)
        match(1)
        pltpu.make_async_copy(received, received, slot_recv).wait()
        for part in range(3):
            total += jnp.dot(spread[part], received[part].reshape(slots, BLK), preferred_element_type=F32)
        final[0:count, :] = final[0:count, :] + dt * total
        write_part(final, out, 0)
        fix(0, 1)


def store(state, aux, state_out, aux_out, sem):
    parts = state.shape[1]
    copies = [
        pltpu.make_async_copy(state.at[:, i], state_out.at[:, i], sem.at[i]) for i in range(parts)
    ]
    copies.append(pltpu.make_async_copy(aux, aux_out, sem.at[parts]))
    for copy in copies:
        copy.start()
    for copy in copies:
        copy.wait()


def shards(tiles, fields, face_aux, block_owner):
    _, parts, rows, depth = fields.shape
    order = face_aux.shape[2]
    count = rows * depth // BLK
    span = rows + 2 * HALO
    vmem = pl.BlockSpec(memory_space=pltpu.VMEM)
    hbm = pl.BlockSpec(memory_space=pltpu.HBM)
    dma = pltpu.SemaphoreType.DMA
    fields, face_aux, block_owner = (
        pltpu.with_memory_space_constraint(a, pltpu.HBM) for a in (fields, face_aux, block_owner)
    )
    in_vmem = lambda *arrays: [pltpu.with_memory_space_constraint(a, pltpu.VMEM) for a in arrays]
    stage = pltpu.VMEM((parts, rows, depth), F32)
    wide = pltpu.VMEM((parts * span * 8, BLK), F32)
    exact = pltpu.VMEM((parts * rows * 8 + 8, BLK), F32)
    halo = pltpu.VMEM((2, parts * HALO * 8, BLK), BF16)
    slots = (tiles, SLOT // 2, 2, BLK)
    names = (tiles, 1, WIDE)
    les, packed, ids = pl.pallas_call(
        functools.partial(les_kernel, tiles),
        out_shape=(
            exact, pltpu.VMEM(slots, BF16),
            pltpu.VMEM(names, F32),
        ),
        in_specs=[hbm, hbm],
        out_specs=(vmem, vmem, vmem),
        scratch_shapes=[
            stage, wide, wide, pltpu.VMEM((1, count), jnp.int32), halo, halo,
            pltpu.VMEM((tiles * SLOT, count), BF16), pltpu.VMEM((count, BLK), BF16),
            pltpu.VMEM((tiles * SLOT, BLK), F32), pltpu.VMEM((2, 8, BLK), F32), dma((3,)), dma, dma((2,)), dma((2,)), dma, dma,
        ],
        compiler_params=pltpu.CompilerParams(
            collective_id=0, has_side_effects=True, vmem_limit_bytes=40 << 20
        ),
    )(fields, block_owner)
    results = pl.pallas_call(
        functools.partial(exchange_kernel, tiles),
        out_shape=(pltpu.VMEM(fields.shape, F32), pltpu.VMEM(face_aux.shape, F32)),
        in_specs=[hbm, hbm, vmem, vmem, vmem],
        out_specs=(vmem, vmem),
        scratch_shapes=[
            stage, wide, exact, pltpu.VMEM((2, order, rows), F32),
            pltpu.VMEM((2, 2, order, rows), F32), halo, halo,
            pltpu.VMEM((2,) + names, F32),
            pltpu.VMEM((3,) + slots, BF16), pltpu.VMEM((3, count, tiles * SLOT), BF16),
            dma((3,)), dma, dma((2,)), dma((2,)), dma((2,)), dma((2,)),
            dma, dma((2,)), dma, dma,
            pltpu.SemaphoreType.REGULAR,
        ],
        compiler_params=pltpu.CompilerParams(
            collective_id=1, has_side_effects=True, vmem_limit_bytes=40 << 20
        ),
    )(fields, face_aux, *in_vmem(les, packed, ids))
    return pl.pallas_call(
        store,
        out_shape=(pltpu.HBM(fields.shape, F32), pltpu.HBM(face_aux.shape, F32)),
        in_specs=[vmem, vmem],
        out_specs=(hbm, hbm),
        scratch_shapes=[dma((parts + 1,))],
    )(*in_vmem(*results))


def solution(mesh):
    return jax.shard_map(
        functools.partial(shards, mesh.shape["tile"]),
        mesh=mesh,
        in_specs=(P("grp", None, "tile", None), P("grp", None, None, "tile"), P("grp", "tile")),
        out_specs=(P("grp", None, "tile", None), P("grp", None, None, "tile")),
        check_vma=False,
    )
```

```python
import functools
import math

import jax
import jax.numpy as jnp
from jax import lax
from jax.experimental import pallas as pl
from jax.experimental.pallas import tpu as pltpu
from jax.sharding import PartitionSpec as P

MESH = pl.DeviceIdType.MESH


def ring(step):
    return min(step, 4 - step)


F32 = jnp.float32
BF16 = jnp.bfloat16

BLK = 128
SLOT = 12
LANES = 16
WIDE = 2 * LANES
COLUMNS = sorted(range(16), key=lambda c: (-ring(c // 4) - ring(c % 4), c))
FAR_COLUMNS = sum(ring(c // 4) + ring(c % 4) > 2 for c in COLUMNS)
HALO = 4

LES_DT = 0.1
VISCOSITY = 1.0
ACOUSTIC_DT = 0.2
MACH = 0.3
TANGENT = 1.0
NEAR = 8.0 * LES_DT / 12.0
FAR = LES_DT / 12.0
DIFF = VISCOSITY * LES_DT


def iota(shape, dim):
    return lax.broadcasted_iota(jnp.int32, shape, dim)


def tile_at(tile, column, step):
    y, x, z = tile // 16, lax.rem(tile // 4, 4), lax.rem(tile, 4)
    y, x = lax.rem(y + column // 4, 4), lax.rem(x + column % 4, 4)
    z = (3 - z, 2 + lax.rem(z, 2) * 2 - z, 1 + z // 2 * 4 - z, z)[step]
    return y * 16 + x * 4 + z


def turn_of(target, tile):
    y, x, z = tile // 16, lax.rem(tile // 4, 4), lax.rem(tile, 4)
    dy = jnp.bitwise_and(lax.shift_right_logical(target, 4) - y, 3)
    dx = jnp.bitwise_and(lax.shift_right_logical(target, 2) - x, 3)
    dz = 3 - jnp.bitwise_xor(jnp.bitwise_and(target, 3), z)
    code = dy * 4 + dx
    place = jnp.zeros_like(code)
    for i, column in enumerate(COLUMNS):
        place = jnp.where(code == column, i, place)
    return place * 4 + dz


def exact_dot(a, b, dims):
    return lax.dot_general(
        a, b, (dims, ((), ())), precision=lax.Precision.HIGHEST, preferred_element_type=F32
    )


def roll(x, shift, axis):
    return pltpu.roll(x, shift % x.shape[axis], axis)


def ahead(one, two):
    lane, sub = iota((1, 8, BLK), 2), iota((1, 8, BLK), 1)
    one, two = roll(one, -1, 2), roll(two, -2, 2)
    own = jnp.where(lane < BLK - 1, one, 0.0) + jnp.where(lane < BLK - 2, two, 0.0)
    cross = jnp.where((lane == BLK - 1) & (sub > 0), one, 0.0) + jnp.where(
        (lane >= BLK - 2) & (sub > 0), two, 0.0
    )
    return own + roll(cross, -1, 1)


def behind(one, two):
    lane, sub = iota((1, 8, BLK), 2), iota((1, 8, BLK), 1)
    one, two = roll(one, 1, 2), roll(two, 2, 2)
    own = jnp.where(lane >= 1, one, 0.0) + jnp.where(lane >= 2, two, 0.0)
    cross = jnp.where((lane == 0) & (sub < 7), one, 0.0) + jnp.where(
        (lane < 2) & (sub < 7), two, 0.0
    )
    return own + roll(cross, 1, 1)


def rows_at(ref, part, row, count, span):
    start = pl.multiple_of((part * span + row) * 8, 8)
    return ref[pl.ds(start, count * 8), :].reshape(count, 8, BLK)


def put_rows(ref, part, row, value, span):
    start = pl.multiple_of((part * span + row) * 8, 8)
    ref[pl.ds(start, value.shape[0] * 8), :] = value.reshape(value.shape[0] * 8, BLK)


def les_rows(src, row, count, span):
    u = rows_at(src, 0, row - 2, count + 4, span)
    w = rows_at(src, 2, row, count, span)
    up, down, far = DIFF - NEAR * u[3:-1], DIFF + NEAR * u[1:-3], FAR * u
    right, left, side = DIFF - NEAR * w, DIFF + NEAR * w, FAR * w
    out = []
    for part in range(4):
        q = rows_at(src, part, row - 2, count + 4, span)
        core, bent = q[2:-2], far * q
        across = up * q[3:-1] + down * q[1:-3] + (bent[4:] - bent[:-4])
        edge = side * core
        along = ahead(right * core, edge) + behind(left * core, -edge)
        out.append((1.0 - 4.0 * DIFF) * core + across + along)
    return out


def source_rows(state):
    mix = state[0] * state[0] - state[2] * state[2] + state[1] * state[3]
    none = jnp.zeros_like(mix)
    quarter = 0.25 * mix
    return ahead(quarter, none) + behind(quarter, none) + 0.5 * mix


def slope_rows(q):
    return (q[:-4] - q[4:] + 8.0 * (q[3:-1] - q[1:-3])) * (1.0 / 12.0)


def slope_depth(q):
    near = (8.0 / 12.0) * q
    far = (1.0 / 12.0) * q
    return ahead(near, -far) + behind(-near, far)


def spread_rows(stage, state, first, count):
    span = state.shape[0] // 32
    for part in range(4):
        for lane in range(8):
            start = (part * span + HALO + first) * 8 + lane
            state[pl.ds(start, count, stride=8), :] = stage[
                part, first : first + count, lane * BLK : (lane + 1) * BLK
            ]


def write_part(final, out, part):
    rows = out.shape[2]
    for lane in range(8):
        out[0, part, :, lane * BLK : (lane + 1) * BLK] = final[
            pl.ds(part * rows * 8 + lane, rows, stride=8), :
        ]


class Halos:
    def __init__(self, tiles, tile, state, halo_out, halo_in, send, recv):
        self.state, self.halo_out, self.halo_in = state, halo_out, halo_in
        self.has_before, self.has_after = tile > 0, tile < tiles - 1
        wheres = (lax.rem(tile + tiles - 1, tiles), lax.rem(tile + 1, tiles))
        self.copies = [
            pltpu.make_async_remote_copy(
                halo_out.at[i], halo_in.at[i], send.at[i], recv.at[i],
                device_id={"tile": where}, device_id_type=MESH,
            )
            for i, where in enumerate(wheres)
        ]
        self.span = state.shape[0] // 32
        self.rows = self.span - 2 * HALO

    def pack(self):
        for part in range(4):
            piece = slice(part * HALO * 8, (part + 1) * HALO * 8)
            low = rows_at(self.state, part, HALO, HALO, self.span)
            high = rows_at(self.state, part, self.rows, HALO, self.span)
            self.halo_out[0, piece] = low.reshape(-1, BLK).astype(BF16)
            self.halo_out[1, piece] = high.reshape(-1, BLK).astype(BF16)

    def start(self):
        for copy, there in zip(self.copies, (self.has_before, self.has_after)):
            pl.when(there)(copy.start)

    def take(self):
        for copy, there in zip(self.copies, (self.has_after, self.has_before)):
            pl.when(there)(copy.wait_recv)
        for part in range(4):
            piece = slice(part * HALO * 8, (part + 1) * HALO * 8)
            upper = jnp.where(self.has_after, self.halo_in[0, piece].astype(F32), 0.0)
            lower = jnp.where(self.has_before, self.halo_in[1, piece].astype(F32), 0.0)
            put_rows(self.state, part, 0, lower.reshape(HALO, 8, BLK), self.span)
            put_rows(self.state, part, self.rows + HALO, upper.reshape(HALO, 8, BLK), self.span)

    def finish(self):
        for copy, there in zip(self.copies, (self.has_before, self.has_after)):
            pl.when(there)(copy.wait_send)


def row_loads(fields, stage, sem):
    rows = stage.shape[1]
    edges = (slice(0, 8), slice(rows - 8, rows), slice(8, rows - 8))
    return [
        pltpu.make_async_copy(fields.at[0, :, part], stage.at[:, part], sem.at[i])
        for i, part in enumerate(edges)
    ]


def les_kernel(
    tiles, fields, owner, final, packed, names,
    stage, state, middle, own, halo_out, halo_in, pack, blocks, inner_slots, ids,
    load_sem, own_sem, halo_send, halo_recv, id_send, id_recv,
):
    rows = stage.shape[1]
    span = rows + 2 * HALO
    group, tile = lax.axis_index("grp"), lax.axis_index("tile")
    last = lax.axis_size("grp") - 1
    halos = Halos(tiles, tile, state, halo_out, halo_in, halo_send, halo_recv)
    barrier = pltpu.get_barrier_semaphore()

    @pl.when(group < last)
    def _():
        loads = row_loads(fields, stage, load_sem)
        own_load = pltpu.make_async_copy(owner, own, own_sem)
        for copy in loads[:2]:
            copy.start()
        own_load.start()
        loads[2].start()

        @pl.when(group < 2)
        def _():
            pl.semaphore_signal(
                barrier, inc=1, device_id={"grp": lax.rem(group + 1, 2)}, device_id_type=MESH
            )

        for there, step in ((halos.has_before, tiles - 1), (halos.has_after, 1)):

            @pl.when(there)
            def _():
                pl.semaphore_signal(
                    barrier, inc=1, device_id={"tile": lax.rem(tile + step, tiles)},
                    device_id_type=MESH,
                )

        loads[0].wait()
        loads[1].wait()
        spread_rows(stage, state, 0, 8)
        spread_rows(stage, state, rows - 8, 8)
        halos.pack()
        paired = group < 2
        neighbours = halos.has_before.astype(jnp.int32) + halos.has_after.astype(jnp.int32)
        neighbours = neighbours + paired.astype(jnp.int32)
        id_copy = pltpu.make_async_remote_copy(
            ids.at[0], ids.at[1], id_send, id_recv,
            device_id={"grp": lax.rem(group + 1, 2)}, device_id_type=MESH,
        )
        chip = lax.rem(tile, 4)

        def meet():
            pl.semaphore_wait(barrier, neighbours)
            halos.start()

        early, late = (group < 2) & (chip == 3), (group < 2) & (chip == 0)
        middling = (group == 2) & ((chip == 0) | (chip == 3))
        pl.when(early)(meet)
        own_load.wait()
        count = own.shape[1]
        owned = own[...]
        live = owned >= 0
        target = lax.shift_right_logical(owned, int(math.log2(count)))
        place = jnp.bitwise_and(owned, count - 1)
        turn = turn_of(target, tile)
        hit = (iota((tiles, count), 0) == turn) & live
        hits = jnp.where(hit, 1.0, 0.0)
        earlier = jnp.where(iota((count, count), 0) < iota((count, count), 1), 1.0, 0.0)
        ranks = jnp.dot(hits.astype(BF16), earlier.astype(BF16), preferred_element_type=F32)
        rank = jnp.sum(hits * ranks, axis=0, keepdims=True).astype(jnp.int32)
        slot = jnp.where(live, turn * SLOT + rank, -1)
        pack[...] = jnp.where(iota((tiles * SLOT, count), 0) == slot, 1.0, 0.0).astype(BF16)
        listed = (iota((8, count), 0) == lax.shift_right_logical(turn, 3)) & live
        high = jnp.where(listed, lax.shift_right_logical(place, 4).astype(F32), 0.0)
        low = jnp.where(listed, (jnp.bitwise_and(place, 15) + 1).astype(F32), 0.0)
        lane = jnp.bitwise_and(turn, 7) * LANES + rank
        chosen = jnp.where(iota((BLK, count), 0) == lane, 1.0, 0.0).astype(BF16)
        digits = lax.dot_general(
            jnp.concatenate([high, low], axis=0).astype(BF16), chosen,
            (((1,), (1,)), ((), ())), preferred_element_type=F32,
        )
        ids[0] = 16.0 * digits[:8] + digits[8:]
        loads[2].wait()
        spread_rows(stage, state, 8, rows - 16)

        def first_step(row, size):
            for part, value in enumerate(les_rows(state, row, size, span)):
                put_rows(middle, part, row, value, span)

        def second_step(row, size):
            values = les_rows(middle, row, size, span)
            for part, value in enumerate(values):
                put_rows(final, part, row - HALO, value, rows)
            start = (row - HALO) * 8
            blocks[start : start + size * 8, :] = source_rows(values).reshape(-1, BLK).astype(BF16)

        pl.when((chip == 1) | (chip == 2))(meet)
        first_step(6, rows - 4)
        pl.when(middling)(meet)
        second_step(8, rows - 8)
        pl.when(late)(meet)
        inner = slice(count // 4, 3 * count // 4)
        inner_slots[...] = jnp.dot(pack[:, inner], blocks[inner], preferred_element_type=F32)
        pl.when(paired)(id_copy.start)
        pl.when(paired)(id_copy.wait_recv)
        turns, lane = iota((tiles, BLK), 0), iota((tiles, BLK), 1)
        chosen_row = jnp.where(iota((tiles, 8), 1) == iota((tiles, 8), 0) // 8, 1.0, 0.0)
        kept = lax.shift_right_logical(lane, 4) == jnp.bitwise_and(turns, 7)
        folded = jnp.bitwise_and(iota((BLK, WIDE), 0), LANES - 1)

        def placed(listed, part):
            listed = jnp.where(kept, exact_dot(chosen_row, listed, ((1,), (0,))), 0.0)
            fold = jnp.where(iota((BLK, WIDE), 1) == folded + part * LANES, 1.0, 0.0)
            return exact_dot(listed, fold, ((1,), (0,)))

        others = jnp.where(paired, ids[1], 0.0)
        listed = placed(ids[0], lax.rem(group, 2)) + placed(others, lax.rem(group + 1, 2))
        names[...] = listed.reshape(tiles, 1, WIDE)

        halos.take()
        tops, bottoms = les_rows(state, 2, 4, span), les_rows(state, rows + 2, 4, span)
        for part in range(4):
            put_rows(middle, part, 2, tops[part], span)
            put_rows(middle, part, rows + 2, bottoms[part], span)
        for part in range(4):
            low_rows = rows_at(middle, part, 2, 2, span)
            put_rows(middle, part, 2, jnp.where(halos.has_before, low_rows, 0.0), span)
            high_rows = rows_at(middle, part, rows + 4, 2, span)
            put_rows(middle, part, rows + 4, jnp.where(halos.has_after, high_rows, 0.0), span)
        tops, bottoms = les_rows(middle, 4, 4, span), les_rows(middle, rows, 4, span)
        for values, row in ((tops, 0), (bottoms, rows - 4)):
            for part in range(4):
                put_rows(final, part, row, values[part], rows)
            start = row * 8
            blocks[start : start + 32, :] = source_rows(values).reshape(-1, BLK).astype(BF16)
        chosen_blocks = inner_slots[...]
        for outer in (slice(0, count // 4), slice(3 * count // 4, count)):
            chosen_blocks += jnp.dot(pack[:, outer], blocks[outer], preferred_element_type=F32)
        packed[...] = chosen_blocks.astype(BF16).reshape(packed.shape)
        halos.finish()
        pl.when(paired)(id_copy.wait_send)


def exchange_kernel(
    tiles, fields, face_aux, les, packed, names, out, aux_out,
    stage, state, final, aux, aux_sides, halo_out, halo_in,
    names_in, received, spread,
    load_sem, aux_sem, halo_send, halo_recv, aux_send, aux_recv,
    name_send, name_recv, slot_send, slot_recv, partner_in,
):
    rows = stage.shape[1]
    span = rows + 2 * HALO
    group, tile = lax.axis_index("grp"), lax.axis_index("tile")
    last = lax.axis_size("grp") - 1
    after, before = lax.rem(tile + 1, tiles), lax.rem(tile + tiles - 1, tiles)
    halos = Halos(tiles, tile, state, halo_out, halo_in, halo_send, halo_recv)
    barrier = pltpu.get_barrier_semaphore()
    far = 4 * FAR_COLUMNS

    half = tiles // 2

    def send(name_turns, order):
        def send_names(turn, which):
            pltpu.make_async_remote_copy(
                names.at[turn], names_in.at[which, turn], name_send, name_recv.at[which],
                device_id=there(COLUMNS[turn // 4], turn % 4), device_id_type=MESH,
            ).start()

        there = lambda c, k: {"grp": last, "tile": tile_at(tile, c, k)}
        which = 1 if len(name_turns) == tiles else 0
        for turn in name_turns:
            send_names(turn, which)
        split = 11
        turns = [4 * place + step for place in range(split) for step in order]
        for part in (order[:2], order[2:]):
            turns += [4 * place + step for place in range(split, 16) for step in part]
        for turn in turns:
            pltpu.make_async_remote_copy(
                packed.at[turn], received.at[group, turn], slot_send, slot_recv,
                device_id=there(COLUMNS[turn // 4], turn % 4), device_id_type=MESH,
            ).start()

    def tell(sem, **there):
        pl.semaphore_signal(sem, inc=1, device_id=there, device_id_type=MESH)

    for mine, heard in ((0, far), (1, tiles - far)):

        @pl.when(group == mine)
        def _():
            tell(barrier, grp=1 - mine)
            pl.semaphore_wait(barrier, heard + 1)
            tell(partner_in, grp=1 - mine)
            pl.semaphore_wait(partner_in, 1)
            if mine == 0:
                pl.when(tile == 0)(lambda: pl.semaphore_wait(partner_in, 1))
            send(range(mine * half, (mine + 1) * half), (2, 1, 3, 0))
            if mine == 1:
                pl.when(tile == 0)(lambda: tell(partner_in, grp=0))
            sent = names.at[pl.ds(0, half)]
            pltpu.make_async_copy(sent, sent, name_send).wait()

    @pl.when(group == 2)
    def _():
        pl.semaphore_wait(barrier, tiles)
        send(range(tiles), range(4))
        pltpu.make_async_copy(names, names, name_send).wait()

    @pl.when(group < last)
    def _():
        for part in range(4):
            write_part(les, out, part)
        aux_load = pltpu.make_async_copy(face_aux.at[0], aux_out.at[0], aux_sem)
        aux_load.start()
        aux_load.wait()
        pltpu.make_async_copy(packed, packed, slot_send).wait()

    @pl.when(group == last)
    def _():
        for where in (before, after):
            pl.semaphore_signal(barrier, inc=1, device_id={"tile": where}, device_id_type=MESH)

        for place, column in enumerate(COLUMNS):

            for step in range(4):
                where = tile_at(tile, column, step)
                tell(barrier, grp=0 if place < FAR_COLUMNS else 1, tile=where)

        for place, column in enumerate(COLUMNS):
            for step in range(4):
                tell(barrier, grp=2, tile=tile_at(tile, column, step))

        loads = row_loads(fields, stage, load_sem)
        aux_load = pltpu.make_async_copy(face_aux.at[0], aux, aux_sem)
        for copy in loads:
            copy.start()
        aux_load.start()
        for copy in loads:
            copy.wait()
        spread_rows(stage, state, 0, rows)
        halos.pack()
        aux_load.wait()
        turns = [
            pltpu.make_async_remote_copy(
                aux, aux_sides.at[i], aux_send.at[i], aux_recv.at[i],
                device_id={"tile": where}, device_id_type=MESH,
            )
            for i, where in ((0, before), (1, after))
        ]
        pl.semaphore_wait(barrier, 2)
        halos.start()
        for copy in turns:
            copy.start()
        halos.take()

        dt = ACOUSTIC_DT

        size = rows // 4

        @pl.loop(0, 4)
        def _(step):
            row = HALO + step * size
            p, u, w, r = (rows_at(state, part, row - 2, size + 4, span) for part in range(4))
            dp, du, dw, dr = (slope_rows(q) for q in (p, u, w, r))
            p, u, w, r = (q[2:-2] for q in (p, u, w, r))
            div = du + slope_depth(w)
            news = (
                p + dt * (-MACH * dp - div),
                u + dt * (-MACH * du - dp),
                w + dt * (-MACH * dw - slope_depth(p)),
                r + dt * (-MACH * dr - div),
            )
            for part, value in enumerate(news):
                put_rows(final, part, step * size, value, rows)

        for copy in turns:
            copy.wait_recv()
        order = aux.shape[1]
        level = iota((order, 1), 0).astype(F32)
        rates = 0.1 * (level + 1.0)
        coupling = 0.5 + 0.5 * jnp.cos(math.pi * (level + 0.5) / order)
        here, there = iota((rows, rows), 0), iota((rows, rows), 1)
        bend = jnp.where(here == there, -2.0, 0.0) + jnp.where(
            (here == there + 1) | (here == there - 1), 1.0, 0.0
        )
        from_after = jnp.where((here == 0) & (there == rows - 1), 1.0, 0.0)
        from_before = jnp.where((here == rows - 1) & (there == 0), 1.0, 0.0)
        lane = iota((8, BLK), 1)
        kind = iota((8, BLK), 0)
        fixes = []
        for face in range(2):
            column = slice(0, BLK) if face == 0 else slice(7 * BLK, 8 * BLK)
            press, vel = stage[0, :, column], stage[2, :, column]
            mixed = 0.5 * (press - vel) if face == 0 else 0.5 * (press + vel)
            pick = jnp.where(lane == (0 if face == 0 else BLK - 1), 1.0, 0.0)
            outgoing = exact_dot(pick, mixed, ((1,), (1,)))[0:1]
            old = aux[face]
            second = (
                exact_dot(old, bend, ((1,), (0,)))
                + exact_dot(aux_sides[0, face], from_after, ((1,), (0,)))
                + exact_dot(aux_sides[1, face], from_before, ((1,), (0,)))
            )
            prior = jnp.concatenate([outgoing, old[:-1]], axis=0)
            new = old + dt * (-rates * old + coupling * (prior - old) + TANGENT * second)
            aux_out[0, face] = new
            incoming = jnp.sum(new, axis=0, keepdims=True) * (1.0 / order)
            ghost_p = outgoing + incoming
            ghost_w = incoming - outgoing if face == 0 else outgoing - incoming
            if face == 0:
                shape = jnp.where(lane == 0, -7.0 / 12.0, 0.0) + jnp.where(lane == 1, 1.0 / 12.0, 0.0)
            else:
                shape = jnp.where(lane == BLK - 1, 7.0 / 12.0, 0.0) + jnp.where(
                    lane == BLK - 2, -1.0 / 12.0, 0.0
                )
            shape = jnp.where(kind == 0, -dt * shape, 0.0)
            wide = [jnp.broadcast_to(g, (8, rows)) for g in (ghost_p, ghost_w)]
            fixes.append([exact_dot(g, shape, ((0,), (0,))) for g in wide])

        def fix(part, which):
            for face, column in ((0, slice(0, BLK)), (1, slice(7 * BLK, 8 * BLK))):
                out[0, part, :, column] = out[0, part, :, column] + fixes[face][which]

        for part in range(1, 4):
            write_part(final, out, part)
        fix(2, 0)
        fix(3, 1)

        for copy in turns:
            copy.wait_send()
        halos.finish()
        count, slots = spread.shape[1:]
        item = iota((1, slots), 1)
        item_turn = lax.shift_right_logical(item * 43691, 19)
        item_rank = item - item_turn * SLOT

        total = jnp.zeros((count, BLK), F32)

        def match(which):
            got = names_in.at[which]
            pltpu.make_async_copy(got, got, name_recv.at[which]).wait()
            listed = names_in[which].reshape(tiles, WIDE)
            for part in ((0, 1), (2,))[which]:
                lane = item_rank + part % 2 * LANES
                column = jnp.where(iota((WIDE, slots), 0) == lane, 1.0, 0.0)
                item_name = exact_dot(listed, column, ((1,), (0,)))
                item_name = jnp.where(iota((tiles, slots), 0) == item_turn, item_name, 0.0)
                item_name = jnp.sum(item_name, axis=0, keepdims=True).astype(jnp.int32) - 1
                same = iota((count, slots), 0) == item_name
                spread[part] = jnp.where(same, 1.0, 0.0).astype(BF16)

        match(0)
        match(1)
        pltpu.make_async_copy(received, received, slot_recv).wait()
        for part in range(3):
            total += jnp.dot(spread[part], received[part].reshape(slots, BLK), preferred_element_type=F32)
        final[0:count, :] = final[0:count, :] + dt * total
        write_part(final, out, 0)
        fix(0, 1)


def store(state, aux, state_out, aux_out, sem):
    parts = state.shape[1]
    copies = [
        pltpu.make_async_copy(state.at[:, i], state_out.at[:, i], sem.at[i]) for i in range(parts)
    ]
    copies.append(pltpu.make_async_copy(aux, aux_out, sem.at[parts]))
    for copy in copies:
        copy.start()
    for copy in copies:
        copy.wait()


def shards(tiles, fields, face_aux, block_owner):
    _, parts, rows, depth = fields.shape
    order = face_aux.shape[2]
    count = rows * depth // BLK
    span = rows + 2 * HALO
    vmem = pl.BlockSpec(memory_space=pltpu.VMEM)
    hbm = pl.BlockSpec(memory_space=pltpu.HBM)
    dma = pltpu.SemaphoreType.DMA
    fields, face_aux, block_owner = (
        pltpu.with_memory_space_constraint(a, pltpu.HBM) for a in (fields, face_aux, block_owner)
    )
    in_vmem = lambda *arrays: [pltpu.with_memory_space_constraint(a, pltpu.VMEM) for a in arrays]
    stage = pltpu.VMEM((parts, rows, depth), F32)
    wide = pltpu.VMEM((parts * span * 8, BLK), F32)
    exact = pltpu.VMEM((parts * rows * 8 + 8, BLK), F32)
    halo = pltpu.VMEM((2, parts * HALO * 8, BLK), BF16)
    slots = (tiles, SLOT // 2, 2, BLK)
    names = (tiles, 1, WIDE)
    les, packed, ids = pl.pallas_call(
        functools.partial(les_kernel, tiles),
        out_shape=(
            exact, pltpu.VMEM(slots, BF16),
            pltpu.VMEM(names, F32),
        ),
        in_specs=[hbm, hbm],
        out_specs=(vmem, vmem, vmem),
        scratch_shapes=[
            stage, wide, wide, pltpu.VMEM((1, count), jnp.int32), halo, halo,
            pltpu.VMEM((tiles * SLOT, count), BF16), pltpu.VMEM((count, BLK), BF16),
            pltpu.VMEM((tiles * SLOT, BLK), F32), pltpu.VMEM((2, 8, BLK), F32), dma((3,)), dma, dma((2,)), dma((2,)), dma, dma,
        ],
        compiler_params=pltpu.CompilerParams(
            collective_id=0, has_side_effects=True, vmem_limit_bytes=40 << 20
        ),
    )(fields, block_owner)
    results = pl.pallas_call(
        functools.partial(exchange_kernel, tiles),
        out_shape=(pltpu.VMEM(fields.shape, F32), pltpu.VMEM(face_aux.shape, F32)),
        in_specs=[hbm, hbm, vmem, vmem, vmem],
        out_specs=(vmem, vmem),
        scratch_shapes=[
            stage, wide, exact, pltpu.VMEM((2, order, rows), F32),
            pltpu.VMEM((2, 2, order, rows), F32), halo, halo,
            pltpu.VMEM((2,) + names, F32),
            pltpu.VMEM((3,) + slots, BF16), pltpu.VMEM((3, count, tiles * SLOT), BF16),
            dma((3,)), dma, dma((2,)), dma((2,)), dma((2,)), dma((2,)),
            dma, dma((2,)), dma, dma,
            pltpu.SemaphoreType.REGULAR,
        ],
        compiler_params=pltpu.CompilerParams(
            collective_id=1, has_side_effects=True, vmem_limit_bytes=40 << 20
        ),
    )(fields, face_aux, *in_vmem(les, packed, ids))
    return pl.pallas_call(
        store,
        out_shape=(pltpu.HBM(fields.shape, F32), pltpu.HBM(face_aux.shape, F32)),
        in_specs=[vmem, vmem],
        out_specs=(hbm, hbm),
        scratch_shapes=[dma((parts + 1,))],
    )(*in_vmem(*results))


def solution(mesh):
    return jax.shard_map(
        functools.partial(shards, mesh.shape["tile"]),
        mesh=mesh,
        in_specs=(P("grp", None, "tile", None), P("grp", None, None, "tile"), P("grp", "tile")),
        out_specs=(P("grp", None, "tile", None), P("grp", None, None, "tile")),
        check_vma=False,
    )
```
